32 devices in a mesh: seq: 32 (over z, y, x, core), mp: 1.
Axes of the slice: x: 2, y: 2, z: 4, core: 2. Of those that a mesh axis runs over, the one named last changes fastest.
Arguments:
- query: bfloat16 [1, 64, 64, 1024], P(None, 'seq', None, 'mp'), may hold values from -6 to 6
- keys: bfloat16 [1, 64, 64, 1024], P(None, 'seq', None, 'mp'), may hold values from -6 to 6
- values: bfloat16 [1, 64, 64, 1024], P(None, 'seq', None, 'mp'), may hold values from -6 to 6
- resid: bfloat16 [1, 64, 64, 1920], P(None, 'seq', 'mp'), may hold values from -4 to 4
- out_weight: bfloat16 [1024, 1920], P('mp'), may hold values from -0.1875 to 0.1875
- norm_gain: float32 [1920], replicated, may hold values from 0.1 to 1.9
- norm_bias: float32 [1920], replicated, may hold values from -3 to 3
- deconv1_weight: bfloat16 [384, 4, 4, 1920], P('mp'), may hold values from -0.0625 to 0.0625
- deconv1_bias: float32 [384], P('mp'), may hold values from -3 to 3
- deconv2_weight: bfloat16 [384, 4, 4, 384], P('mp'), may hold values from -0.15625 to 0.15625
- deconv2_bias: float32 [384], P('mp'), may hold values from -3 to 3
- final_weight: bfloat16 [384, 308], replicated, may hold values from -0.3125 to 0.3125
- final_bias: float32 [308], replicated, may hold values from -3 to 3
Outputs:
- heatmaps: bfloat16 [1, 256, 256, 308], P(None, 'seq', 'mp')
The draws below stay inside these ranges and needn't reach their ends.
All inputs are finite; a program needn't handle non-finite values.
Results may differ from the reference program's by a relative error of at most 0.012.
Values may be sent and summed in bfloat16 or wider, within the bound.
No kernel may reach another device: no remote copies, remote signals or barrier semaphores. Data moves between devices by JAX's collectives and lax.ppermute only.
A program may use at most 256 MiB of HBM per device.

```python
import jax
import jax.numpy as jnp
from jax import lax

D = 1920
HEADS = 16
HEAD_DIM = 64
CHANNELS = 384
KEYPOINTS = 308
GRID = 64
FRAMES = 1


def draw_query(key, part):
    base = jax.random.normal(jax.random.fold_in(key, 11), (FRAMES, GRID, GRID, HEADS * HEAD_DIM), jnp.float32) * 1.4
    base = jnp.clip(base, -6.0, 6.0)
    return base.astype(jnp.bfloat16)


def draw_keys(key, part):
    base = jax.random.normal(jax.random.fold_in(key, 12), (FRAMES, GRID, GRID, HEADS * HEAD_DIM), jnp.float32) * 1.4
    base = jnp.clip(base, -6.0, 6.0)
    return base.astype(jnp.bfloat16)


def levels(own_key, shape, split, smallest, high):
    gain, own = 1.0, jax.random.fold_in(own_key, 6)
    for dim, shards_of in split:
        draws = jnp.exp(jax.random.uniform(jax.random.fold_in(own, dim), (shards_of,), jnp.float32, smallest / len(split), high / len(split)))
        gain = gain * jnp.repeat(draws, shape[dim] // shards_of).reshape([-1 if axis == dim else 1 for axis in range(len(shape))])
    return gain


def gaussian(stream_key, shape, deviation, bound, shards=(), dtype=jnp.bfloat16):
    entries = deviation * jax.random.normal(stream_key, shape, jnp.float32)
    if shards:
        entries = entries * levels(stream_key, shape, shards, -0.22, 0.18)
    return jnp.clip(entries, -bound, bound).astype(dtype)


def setup_inputs(seed: int = 0) -> dict:
    seeds = jax.random.split(jax.random.key(seed), 14)
    query = draw_query(jax.random.fold_in(seeds[13], 71), 0)
    keys = draw_keys(jax.random.fold_in(seeds[13], 71), 0)
    values = gaussian(seeds[2], (FRAMES, GRID, GRID, HEADS * HEAD_DIM), 1.0, 6.0, ((1, 32),))
    resid = gaussian(seeds[3], (FRAMES, GRID, GRID, D), 0.3, 4.0, ((1, 32),))
    out_weight = gaussian(seeds[4], (HEADS * HEAD_DIM, D), (HEADS * HEAD_DIM) ** -0.5, 0.1875)
    norm_gain = jnp.clip(1.0 + 0.18 * jax.random.normal(seeds[5], (D,), jnp.float32), 0.1, 1.9)
    norm_bias = gaussian(seeds[6], (D,), 0.5, 3.0, (), jnp.float32)
    deconv1_weight = gaussian(seeds[7], (CHANNELS, 4, 4, D), (4 * D) ** -0.5, 0.0625)
    deconv1_bias = gaussian(seeds[8], (CHANNELS,), 0.5, 3.0, (), jnp.float32)
    deconv2_weight = gaussian(seeds[9], (CHANNELS, 4, 4, CHANNELS), (4 * CHANNELS) ** -0.5, 0.15625)
    deconv2_bias = gaussian(seeds[10], (CHANNELS,), 0.5, 3.0, (), jnp.float32)
    final_weight = gaussian(seeds[11], (CHANNELS, KEYPOINTS), CHANNELS ** -0.5, 0.3125)
    final_bias = gaussian(seeds[12], (KEYPOINTS,), 0.5, 3.0, (), jnp.float32)
    return {"query": query, "keys": keys, "values": values, "resid": resid, "out_weight": out_weight, "norm_gain": norm_gain, "norm_bias": norm_bias, "deconv1_weight": deconv1_weight, "deconv1_bias": deconv1_bias, "deconv2_weight": deconv2_weight, "deconv2_bias": deconv2_bias, "final_weight": final_weight, "final_bias": final_bias}


TAP_TABLE = (((1, 1), (0, 3)), ((2, 0), (1, 2)))
EPSILON = 1e-06

def tap_product(window, weight, kernel_row, kernel_col):
    tap = weight[:, kernel_row, kernel_col, :]
    return lax.dot_general(window, tap, (((3,), (1,)), ((), ())), preferred_element_type=jnp.float32)

def half_rows(padded, weight, tap_pairs, first_row, row_count):
    col_count = padded.shape[2] - 2
    halves = []
    for col_parity in range(2):
        summed = None
        for pad_row, kernel_row in tap_pairs:
            for pad_col, kernel_col in TAP_TABLE[col_parity]:
                window = padded[:, first_row + pad_row:first_row + pad_row + row_count, pad_col:pad_col + col_count, :]
                product = tap_product(window, weight, kernel_row, kernel_col)
                summed = product if summed is None else summed + product
        halves.append(summed)
    stacked = jnp.stack(halves, axis=3)
    return stacked.reshape(stacked.shape[0], row_count, 2 * col_count, stacked.shape[-1])

def upsample(padded, weight, row_count):
    even_rows = half_rows(padded, weight, TAP_TABLE[0], 0, row_count)
    odd_rows = half_rows(padded, weight, TAP_TABLE[1], 0, row_count)
    stacked = jnp.stack([even_rows, odd_rows], axis=2)
    return stacked.reshape(stacked.shape[0], 2 * row_count, stacked.shape[3], stacked.shape[4])

def pad_grid(field):
    return jnp.pad(field, ((0, 0), (1, 1), (1, 1), (0, 0)))

def layer_norm(stream, norm_gain, norm_bias):
    center = lax.optimization_barrier(jnp.mean(stream, axis=-1, keepdims=True))
    shifted = stream - center
    variance = lax.optimization_barrier(jnp.mean(shifted * shifted, axis=-1, keepdims=True))
    return (shifted * lax.rsqrt(variance + EPSILON) * norm_gain + norm_bias).astype(jnp.bfloat16)

def reference(query, keys, values, resid, out_weight, norm_gain, norm_bias, deconv1_weight, deconv1_bias, deconv2_weight, deconv2_bias, final_weight, final_bias):
    token_count = GRID * GRID
    score_scale = HEAD_DIM ** (-0.5)

    def by_head(field):
        return jnp.transpose(field.reshape(FRAMES, token_count, HEADS, HEAD_DIM), (2, 0, 1, 3))

    def one_head(operands):
        query_head, key_head, value_head = operands
        scores = jnp.einsum('fqd,fkd->fqk', query_head.astype(jnp.float32), key_head.astype(jnp.float32), precision=lax.Precision.HIGHEST) * score_scale
        row_max = lax.optimization_barrier(jnp.max(scores, axis=-1, keepdims=True))
        exps = jnp.exp(scores - row_max)
        denominator = lax.optimization_barrier(jnp.sum(exps, axis=-1, keepdims=True))
        weights = lax.optimization_barrier(exps.astype(jnp.bfloat16))
        mixed = jnp.einsum('fqk,fkd->fqd', weights.astype(jnp.float32), value_head.astype(jnp.float32), precision=lax.Precision.HIGHEST)
        return (mixed / denominator).astype(jnp.bfloat16)
    attended = lax.map(one_head, (by_head(query), by_head(keys), by_head(values)))
    attended = jnp.transpose(attended, (1, 2, 0, 3)).reshape(FRAMES, GRID, GRID, HEADS * HEAD_DIM)
    stream = resid.astype(jnp.float32) + jnp.dot(attended, out_weight, preferred_element_type=jnp.float32)
    normed = layer_norm(stream, norm_gain, norm_bias)
    hidden_one = jnp.maximum(upsample(pad_grid(normed), deconv1_weight, GRID) + deconv1_bias, 0.0).astype(jnp.bfloat16)
    hidden_two = jnp.maximum(upsample(pad_grid(hidden_one), deconv2_weight, 2 * GRID) + deconv2_bias, 0.0).astype(jnp.bfloat16)
    return (jnp.dot(hidden_two, final_weight, preferred_element_type=jnp.float32) + final_bias).astype(jnp.bfloat16)
```

```python
import functools

import jax
import jax.numpy as jnp
from jax import lax
from jax.experimental import pallas as pl
from jax.experimental.pallas import tpu as pltpu
from jax.sharding import PartitionSpec as P

HEAD_DIM = 64


TAP_TABLE = (((1, 1), (0, 3)), ((2, 0), (1, 2)))
EPSILON = 1e-06


def with_halo(array, sides, width):
    for axis, dim in sides:
        size, length = (lax.axis_size(axis), array.shape[dim])
        up = [(i, (i + 1) % size) for i in range(size - 1)]
        down = [(j, i) for i, j in up]
        last = lax.slice_in_dim(array, length - width, length, axis=dim)
        first = lax.slice_in_dim(array, 0, width, axis=dim)
        before = lax.ppermute(last, axis, up)
        after = lax.ppermute(first, axis, down)
        array = jnp.concatenate([before, array, after], axis=dim)
    return array


def tap_product(window, weight, kernel_row, kernel_col):
    tap = weight[:, kernel_row, kernel_col, :]
    return lax.dot_general(
        window, tap, (((3,), (1,)), ((), ())), preferred_element_type=jnp.float32
    )


def half_rows(padded, weight, tap_pairs, first_row, row_count):
    col_count = padded.shape[2] - 2
    halves = []
    for col_parity in range(2):
        summed = None
        for pad_row, kernel_row in tap_pairs:
            for pad_col, kernel_col in TAP_TABLE[col_parity]:
                window = padded[
                    :,
                    first_row + pad_row : first_row + pad_row + row_count,
                    pad_col : pad_col + col_count,
                    :,
                ]
                product = tap_product(window, weight, kernel_row, kernel_col)
                summed = product if summed is None else summed + product
        halves.append(summed)
    stacked = jnp.stack(halves, axis=3)
    return stacked.reshape(stacked.shape[0], row_count, 2 * col_count, stacked.shape[-1])


def upsample(padded, weight, row_count):
    even_rows = half_rows(padded, weight, TAP_TABLE[0], 0, row_count)
    odd_rows = half_rows(padded, weight, TAP_TABLE[1], 0, row_count)
    stacked = jnp.stack([even_rows, odd_rows], axis=2)
    return stacked.reshape(stacked.shape[0], 2 * row_count, stacked.shape[3], stacked.shape[4])


def pad_columns(field):
    return jnp.pad(field, ((0, 0), (0, 0), (1, 1), (0, 0)))


def layer_norm(stream, norm_gain, norm_bias):
    center = jnp.mean(stream, axis=-1, keepdims=True)
    shifted = stream - center
    variance = jnp.mean(shifted * shifted, axis=-1, keepdims=True)
    return (shifted * lax.rsqrt(variance + EPSILON) * norm_gain + norm_bias).astype(jnp.bfloat16)


def local(
    query,
    keys,
    values,
    resid,
    out_weight,
    norm_gain,
    norm_bias,
    deconv1_weight,
    deconv1_bias,
    deconv2_weight,
    deconv2_bias,
    final_weight,
    final_bias,
):
    frame_count, row_count, col_count, feature_width = query.shape
    local_heads = feature_width // HEAD_DIM
    score_scale = HEAD_DIM ** (-0.5)
    query_count = row_count * col_count
    queries = query.reshape(frame_count, query_count, local_heads, HEAD_DIM)
    start_max = jnp.full((frame_count, query_count, local_heads), -1e30, jnp.float32)
    running_max = start_max
    key_piece = lax.all_gather(keys, "seq", axis=1, tiled=True).reshape(
        frame_count, -1, local_heads, HEAD_DIM
    )
    value_piece = lax.all_gather(values, "seq", axis=1, tiled=True).reshape(
        frame_count, -1, local_heads, HEAD_DIM
    )
    scores = (
        jnp.einsum("fqhd,fkhd->fqhk", queries, key_piece, preferred_element_type=jnp.float32)
        * score_scale
    )
    fresh_max = jnp.maximum(running_max, jnp.max(scores, axis=-1))
    exps = jnp.exp(scores - fresh_max[..., None])
    denominator = jnp.sum(exps, axis=-1)
    weighted = jnp.einsum(
        "fqhk,fkhd->fqhd",
        exps.astype(jnp.bfloat16),
        value_piece,
        preferred_element_type=jnp.float32,
    )
    running_max, denominator, weighted = (fresh_max, denominator, weighted)
    attended = (
        (weighted / denominator[..., None])
        .astype(jnp.bfloat16)
        .reshape(frame_count, row_count, col_count, feature_width)
    )
    partial_value = jnp.dot(attended, out_weight, preferred_element_type=jnp.float32)
    summed = lax.psum(partial_value.astype(jnp.bfloat16), "mp").astype(jnp.float32)
    full_resid = lax.all_gather(resid, "mp", axis=2, tiled=True)
    normed = layer_norm(full_resid.astype(jnp.float32) + summed, norm_gain, norm_bias)
    rimmed = with_halo(normed, (("seq", 1),), 1)
    padded = pad_columns(rimmed)
    deconv_one = upsample(padded, deconv1_weight, row_count)
    hidden_one = jnp.maximum(deconv_one + deconv1_bias, 0.0).astype(jnp.bfloat16)
    gathered = lax.all_gather(hidden_one, "mp", axis=3, tiled=True)
    middle = with_halo(gathered, (("seq", 1),), 1)
    deconv_two = upsample(pad_columns(middle), deconv2_weight, 2 * row_count)
    hidden_two = jnp.maximum(deconv_two + deconv2_bias, 0.0).astype(jnp.bfloat16)
    return (
        jnp.dot(
            lax.all_to_all(hidden_two, "mp", split_axis=2, concat_axis=3, tiled=True),
            final_weight,
            preferred_element_type=jnp.float32,
        )
        + final_bias
    ).astype(jnp.bfloat16)

LOG2E = 1.4426950408889634
MIB = 1024 * 1024
NT = (((1,), (1,)), ((), ()))


def dot_nt(left, right):
    return lax.dot_general(left, right, NT, preferred_element_type=jnp.float32)


def whole(shape):
    return pl.BlockSpec(shape, lambda *_: (0,) * len(shape))


def pack_kernel(query_ref, keys_ref, values_ref, out_ref):
    for head in range(out_ref.shape[0] // 2):
        lanes = pl.ds(128 * (head // 2), 128)
        half = head % 2
        own = slice(64 * half, 64 * half + 64)
        for row in range(2):
            block = out_ref.at[2 * head + row]
            queries = query_ref[row, :, lanes][:, own]
            block[0:32, :] = jnp.concatenate([queries[0:32], queries[32:64]], axis=1)
            block[32:96, :] = jnp.concatenate(
                [keys_ref[row, :, lanes][:, own], values_ref[row, :, lanes][:, own]], axis=1
            )


def pack_tokens(query, keys, values, device_count):
    return pl.pallas_call(
        pack_kernel,
        out_shape=jax.ShapeDtypeStruct((device_count, 96, 128), jnp.bfloat16),
        compiler_params=pltpu.CompilerParams(vmem_limit_bytes=16 * MIB),
        name="pack_tokens",
    )(query[0], keys[0], values[0])


def attend_kernel(own_ref, other_ref, out_ref, pairs_ref, *, sources, chunk):
    half = pairs_ref.shape[0] // 2

    @pl.when(pl.program_id(0) == 0)
    def _():
        pairs_ref[0:half, :] = own_ref[:, 32:96, :].reshape(half, 128)
        pairs_ref[half : 2 * half, :] = other_ref[...].reshape(half, 128)

    first = pl.program_id(0) * sources
    packed = own_ref[pl.ds(first, sources), 0:32, :].reshape(sources * 32, 128)
    lane = lax.broadcasted_iota(jnp.int32, packed.shape, 1)
    wide = packed.astype(jnp.float32) * HEAD_DIM ** (-0.5)
    low = jnp.where(lane < 64, wide, 0.0)
    high = jnp.where(lane < 64, pltpu.roll(wide, 64, 1), 0.0)
    queries = jnp.concatenate([low, high], axis=0).astype(jnp.bfloat16)
    top = None
    for start in range(0, 2 * half, chunk):
        pairs = pairs_ref[start : start + chunk, :]
        scores = dot_nt(queries, pairs)
        chunk_top = jnp.max(scores, axis=1, keepdims=True)
        fresh = chunk_top if top is None else jnp.maximum(top, chunk_top)
        exps = jnp.exp2((scores - fresh) * LOG2E)
        part = jnp.sum(exps, axis=1, keepdims=True)
        mixed = jnp.dot(exps.astype(jnp.bfloat16), pairs, preferred_element_type=jnp.float32)
        if top is None:
            total, weighted = part, mixed
        else:
            shrink = jnp.exp2((top - fresh) * LOG2E)
            total = total * shrink + part
            weighted = weighted * shrink + mixed
        top = fresh
    weighted = weighted / total
    rows = sources * 32
    joined = jnp.where(lane < 64, pltpu.roll(weighted[:rows], 64, 1), weighted[rows:])
    out_ref[...] = joined.astype(jnp.bfloat16).reshape(sources, 32, 128)


def attend(own, other, sources=4, chunk=1024):
    count = own.shape[0]
    return pl.pallas_call(
        functools.partial(attend_kernel, sources=sources, chunk=chunk),
        grid=(count // sources,),
        in_specs=[whole(own.shape), whole(other.shape)],
        out_specs=pl.BlockSpec((sources, 32, 128), lambda i: (i, 0, 0)),
        out_shape=jax.ShapeDtypeStruct((count, 32, 128), jnp.bfloat16),
        scratch_shapes=[pltpu.VMEM((2 * count * 64, 128), jnp.bfloat16)],
        compiler_params=pltpu.CompilerParams(vmem_limit_bytes=32 * MIB),
        name="attend",
    )(own, other)


def shift_columns(field, row_length):
    count = field.shape[0]
    column = lax.broadcasted_iota(jnp.int32, field.shape, 0) % row_length
    before = jnp.where(column == 0, 0.0, pltpu.roll(field, 1, 0))
    after = jnp.where(column == row_length - 1, 0.0, pltpu.roll(field, count - 1, 0))
    return before, after


def norm_kernel(inside_ref, mixed_ref, resid_ref, above_ref, below_ref, weight_ref, gain_ref, bias_ref, out_ref):
    width = out_ref.shape[2]
    heads = mixed_ref.shape[0]
    for place, (parity, which) in enumerate(((1, 0), (0, 0), (1, 1), (0, 1))):
        low, high = [], []
        for head in range(0, heads, 2):
            left, right = mixed_ref[head, parity, which], mixed_ref[head + 1, parity, which]
            low.append(jnp.concatenate([left[:, :64], right[:, :64]], axis=1))
            high.append(jnp.concatenate([left[:, 64:], right[:, 64:]], axis=1))
        attended = jnp.concatenate(
            [jnp.concatenate(low, axis=1), jnp.concatenate(high, axis=1)], axis=0
        )
        resid = above_ref[...] if place == 0 else below_ref[...] if place == 3 else resid_ref[place - 1]
        stream = resid.astype(jnp.float32) + jnp.dot(
            attended, weight_ref[...], preferred_element_type=jnp.float32
        )
        center = jnp.mean(stream, axis=-1, keepdims=True)
        shifted = stream - center
        variance = jnp.mean(shifted * shifted, axis=-1, keepdims=True)
        normed = shifted * lax.rsqrt(variance + EPSILON) * gain_ref[...] + bias_ref[...]
        if place in (0, 3):
            normed = jnp.where(inside_ref[place // 3] > 0, normed, 0.0)
        before, after = shift_columns(normed, 64)
        rows = slice(64 * place, 64 * place + 64)
        out_ref[0, rows, :] = before.astype(jnp.bfloat16)
        out_ref[1, rows, :] = normed.astype(jnp.bfloat16)
        out_ref[2, rows, :] = after.astype(jnp.bfloat16)


def project_and_norm(inside, mixed, resid, above, below, out_weight, gain, bias):
    width = resid.shape[-1]
    return pl.pallas_call(
        norm_kernel,
        in_specs=[pl.BlockSpec(memory_space=pltpu.SMEM)] + [pl.BlockSpec(memory_space=pltpu.VMEM)] * 7,
        out_shape=jax.ShapeDtypeStruct((3, 256, width), jnp.bfloat16),
        compiler_params=pltpu.CompilerParams(vmem_limit_bytes=32 * MIB),
        name="project_and_norm",
    )(inside, mixed, resid, above, below, out_weight, gain.reshape(1, -1), bias.reshape(1, -1))


def store_strided(wide_ref, start, value):
    for group in range(wide_ref.shape[0]):
        lanes = slice(128 * group, 128 * group + 128)
        wide_ref[group, pl.ds(start, value.shape[0], stride=2), :] = value[:, lanes]


def load_wide(wide_ref, rows):
    groups = [wide_ref[group, rows, :] for group in range(wide_ref.shape[0])]
    return jnp.concatenate(groups, axis=1).astype(jnp.bfloat16)


def column_taps(parity):
    return ((1, 1), (0, 3)) if parity == 0 else ((1, 2), (2, 0))


def deconv_one_kernel(inside_ref, field_ref, left_ref, right_ref, bias_ref, out_ref, sums_ref, wide_ref):
    step = pl.program_id(0)
    for index in range(8):

        @pl.when(step == index)
        def _():
            row_parity, which, parity = index // 4, (index // 2) % 2, index % 2
            low = (64, 0)[which] if row_parity == 0 else (0, 64)[which]
            field = [field_ref[copy, low : low + 192, :] for copy, _ in column_taps(parity)]
            product = dot_nt(field[0], left_ref[0, 0]) + dot_nt(field[1], right_ref[0, 0])
            if which == 0:
                sums_ref[parity] = product
            else:
                hidden = jnp.maximum(sums_ref[parity] + product + bias_ref[...], 0.0)
                for place in range(3):
                    row = 2 * place + (1 if row_parity == 0 else 0)
                    value = hidden[64 * place : 64 * place + 64]
                    if row == 0:
                        value = jnp.where(inside_ref[0] > 0, value, 0.0)
                    if row == 5:
                        value = jnp.where(inside_ref[1] > 0, value, 0.0)
                    store_strided(wide_ref, 128 * row + parity, value)
            if index == 7:
                out_ref[...] = load_wide(wide_ref, slice(None))


def kernel_row_of(step):
    pair = step // 2
    return jnp.where(pair == 0, 1, jnp.where(pair == 1, 3, jnp.where(pair == 2, 2, 0)))


def deconv_one(inside, field, weight, bias):
    channels, width = weight.shape[2:]
    tap = (1, 1, channels, width)
    return pl.pallas_call(
        deconv_one_kernel,
        grid=(8,),
        in_specs=[
            pl.BlockSpec(memory_space=pltpu.SMEM),
            whole(field.shape),
            pl.BlockSpec(tap, lambda i: (kernel_row_of(i), 1 + i % 2, 0, 0)),
            pl.BlockSpec(tap, lambda i: (kernel_row_of(i), 3 - 3 * (i % 2), 0, 0)),
            whole((1, channels)),
        ],
        out_specs=whole((768, channels)),
        out_shape=jax.ShapeDtypeStruct((768, channels), jnp.bfloat16),
        scratch_shapes=[
            pltpu.VMEM((2, 192, channels), jnp.float32),
            pltpu.VMEM((channels // 128, 768, 128), jnp.float32),
        ],
        compiler_params=pltpu.CompilerParams(vmem_limit_bytes=32 * MIB),
        name="deconv_one",
    )(inside, field, weight, weight, bias.reshape(1, -1))


def deconv_two_kernel(field_ref, weight_ref, bias_ref, final_ref, final_bias_ref, out_ref, copies_ref, wide_ref):
    channels = field_ref.shape[1]
    field = field_ref[...].astype(jnp.float32)
    before, after = shift_columns(field, 128)
    copies_ref[:, 0:channels] = before.astype(jnp.bfloat16)
    copies_ref[:, channels : 2 * channels] = field_ref[...]
    copies_ref[:, 2 * channels :] = after.astype(jnp.bfloat16)
    for row_parity in range(2):
        for parity in range(2):
            total = None
            for low, kernel_row in (((128, 1), (0, 3)), ((128, 2), (256, 0)))[row_parity]:
                for copy, kernel_col in column_taps(parity):
                    product = dot_nt(
                        copies_ref[low : low + 512, copy * channels : (copy + 1) * channels],
                        weight_ref[kernel_row, kernel_col],
                    )
                    total = product if total is None else total + product
            hidden = jnp.maximum(total + bias_ref[...], 0.0)
            for place in range(4):
                start = 256 * (2 * place + row_parity) + parity
                store_strided(wide_ref, start, hidden[128 * place : 128 * place + 128])
    for row in range(8):
        hidden = load_wide(wide_ref, slice(256 * row, 256 * row + 256))
        heat = dot_nt(final_ref[...], hidden) + final_bias_ref[...]
        out_ref[row] = heat.astype(jnp.bfloat16)


def deconv_two(field, weight, bias, final_weight, final_bias):
    channels = field.shape[1]
    keypoints = final_weight.shape[1]
    return pl.pallas_call(
        deconv_two_kernel,
        out_shape=jax.ShapeDtypeStruct((8, keypoints, 256), jnp.bfloat16),
        scratch_shapes=[
            pltpu.VMEM((768, 3 * channels), jnp.bfloat16),
            pltpu.VMEM((channels // 128, 2048, 128), jnp.float32),
        ],
        compiler_params=pltpu.CompilerParams(vmem_limit_bytes=32 * MIB),
        name="deconv_two",
    )(field, weight, bias.reshape(1, -1), final_weight.T, final_bias.reshape(-1, 1))


def by_heads(
    query,
    keys,
    values,
    resid,
    out_weight,
    norm_gain,
    norm_bias,
    deconv1_weight,
    deconv1_bias,
    deconv2_weight,
    deconv2_bias,
    final_weight,
    final_bias,
):
    count = lax.axis_size("seq")
    place = lax.axis_index("seq")
    up = [(i, i + 1) for i in range(count - 1)]
    down = [(i + 1, i) for i in range(count - 1)]
    swap = [(i, i ^ 1) for i in range(count)]

    packed = pack_tokens(query, keys, values, count)
    own = lax.all_to_all(packed, "seq", 0, 0, tiled=True)
    above = lax.ppermute(resid[0, 1], "seq", up)
    below = lax.ppermute(resid[0, 0], "seq", down)
    taps_one = jnp.transpose(deconv1_weight, (1, 2, 0, 3))
    taps_two = jnp.transpose(deconv2_weight, (1, 2, 0, 3))
    other = lax.ppermute(own[:, 32:96], "seq", swap)
    mixed = attend(own, other)

    rim = jnp.zeros((1, 32, 128), jnp.bfloat16)
    earlier = jnp.concatenate([rim, mixed[:-1]], axis=0)
    later = jnp.concatenate([mixed[1:], rim], axis=0)
    odd = place % 2 == 1
    sent = jnp.stack([jnp.where(odd, earlier, mixed), jnp.where(odd, mixed, later)], axis=1)
    back = lax.all_to_all(sent, "seq", 0, 0, tiled=True)
    back = back.reshape(count // 2, 2, 2, 32, 128)

    inside = jnp.stack([place > 0, place < count - 1]).astype(jnp.int32)
    field = project_and_norm(inside, back, resid[0], above, below, out_weight, norm_gain, norm_bias)
    hidden_one = deconv_one(inside, field, taps_one, deconv1_bias)
    heat = deconv_two(hidden_one, taps_two, deconv2_bias, final_weight, final_bias)
    return jnp.transpose(heat, (0, 2, 1))[None]


def step(*arrays):
    query = arrays[0]
    frames, rows, columns, width = query.shape
    heads = width // HEAD_DIM
    whole_heads = lax.axis_size("mp") == 1 and lax.axis_size("seq") == 2 * heads
    if whole_heads and (frames, rows, columns) == (1, 2, 64):
        return by_heads(*arrays)
    return local(*arrays)


def solution(mesh):
    placed = (
        P(None, "seq", None, "mp"),
        P(None, "seq", None, "mp"),
        P(None, "seq", None, "mp"),
        P(None, "seq", "mp", None),
        P("mp", None),
        P(),
        P(),
        P("mp", None, None, None),
        P("mp"),
        P("mp", None, None, None),
        P("mp"),
        P(),
        P(),
    )
    return jax.shard_map(
        step, mesh=mesh, in_specs=placed, out_specs=P(None, "seq", "mp", None), check_vma=False
    )
```

```python
import functools

import jax
import jax.numpy as jnp
from jax import lax
from jax.experimental import pallas as pl
from jax.experimental.pallas import tpu as pltpu
from jax.sharding import PartitionSpec as P

HEAD_DIM = 64


TAP_TABLE = (((1, 1), (0, 3)), ((2, 0), (1, 2)))
EPSILON = 1e-06


def with_halo(array, sides, width):
    for axis, dim in sides:
        size, length = (lax.axis_size(axis), array.shape[dim])
        up = [(i, (i + 1) % size) for i in range(size - 1)]
        down = [(j, i) for i, j in up]
        last = lax.slice_in_dim(array, length - width, length, axis=dim)
        first = lax.slice_in_dim(array, 0, width, axis=dim)
        before = lax.ppermute(last, axis, up)
        after = lax.ppermute(first, axis, down)
        array = jnp.concatenate([before, array, after], axis=dim)
    return array


def tap_product(window, weight, kernel_row, kernel_col):
    tap = weight[:, kernel_row, kernel_col, :]
    return lax.dot_general(
        window, tap, (((3,), (1,)), ((), ())), preferred_element_type=jnp.float32
    )


def half_rows(padded, weight, tap_pairs, first_row, row_count):
    col_count = padded.shape[2] - 2
    halves = []
    for col_parity in range(2):
        summed = None
        for pad_row, kernel_row in tap_pairs:
            for pad_col, kernel_col in TAP_TABLE[col_parity]:
                window = padded[
                    :,
                    first_row + pad_row : first_row + pad_row + row_count,
                    pad_col : pad_col + col_count,
                    :,
                ]
                product = tap_product(window, weight, kernel_row, kernel_col)
                summed = product if summed is None else summed + product
        halves.append(summed)
    stacked = jnp.stack(halves, axis=3)
    return stacked.reshape(stacked.shape[0], row_count, 2 * col_count, stacked.shape[-1])


def upsample(padded, weight, row_count):
    even_rows = half_rows(padded, weight, TAP_TABLE[0], 0, row_count)
    odd_rows = half_rows(padded, weight, TAP_TABLE[1], 0, row_count)
    stacked = jnp.stack([even_rows, odd_rows], axis=2)
    return stacked.reshape(stacked.shape[0], 2 * row_count, stacked.shape[3], stacked.shape[4])


def pad_columns(field):
    return jnp.pad(field, ((0, 0), (0, 0), (1, 1), (0, 0)))


def layer_norm(stream, norm_gain, norm_bias):
    center = jnp.mean(stream, axis=-1, keepdims=True)
    shifted = stream - center
    variance = jnp.mean(shifted * shifted, axis=-1, keepdims=True)
    return (shifted * lax.rsqrt(variance + EPSILON) * norm_gain + norm_bias).astype(jnp.bfloat16)


def local(
    query,
    keys,
    values,
    resid,
    out_weight,
    norm_gain,
    norm_bias,
    deconv1_weight,
    deconv1_bias,
    deconv2_weight,
    deconv2_bias,
    final_weight,
    final_bias,
):
    frame_count, row_count, col_count, feature_width = query.shape
    local_heads = feature_width // HEAD_DIM
    score_scale = HEAD_DIM ** (-0.5)
    query_count = row_count * col_count
    queries = query.reshape(frame_count, query_count, local_heads, HEAD_DIM)
    start_max = jnp.full((frame_count, query_count, local_heads), -1e30, jnp.float32)
    running_max = start_max
    key_piece = lax.all_gather(keys, "seq", axis=1, tiled=True).reshape(
        frame_count, -1, local_heads, HEAD_DIM
    )
    value_piece = lax.all_gather(values, "seq", axis=1, tiled=True).reshape(
        frame_count, -1, local_heads, HEAD_DIM
    )
    scores = (
        jnp.einsum("fqhd,fkhd->fqhk", queries, key_piece, preferred_element_type=jnp.float32)
        * score_scale
    )
    fresh_max = jnp.maximum(running_max, jnp.max(scores, axis=-1))
    exps = jnp.exp(scores - fresh_max[..., None])
    denominator = jnp.sum(exps, axis=-1)
    weighted = jnp.einsum(
        "fqhk,fkhd->fqhd",
        exps.astype(jnp.bfloat16),
        value_piece,
        preferred_element_type=jnp.float32,
    )
    running_max, denominator, weighted = (fresh_max, denominator, weighted)
    attended = (
        (weighted / denominator[..., None])
        .astype(jnp.bfloat16)
        .reshape(frame_count, row_count, col_count, feature_width)
    )
    partial_value = jnp.dot(attended, out_weight, preferred_element_type=jnp.float32)
    summed = lax.psum(partial_value.astype(jnp.bfloat16), "mp").astype(jnp.float32)
    full_resid = lax.all_gather(resid, "mp", axis=2, tiled=True)
    normed = layer_norm(full_resid.astype(jnp.float32) + summed, norm_gain, norm_bias)
    rimmed = with_halo(normed, (("seq", 1),), 1)
    padded = pad_columns(rimmed)
    deconv_one = upsample(padded, deconv1_weight, row_count)
    hidden_one = jnp.maximum(deconv_one + deconv1_bias, 0.0).astype(jnp.bfloat16)
    gathered = lax.all_gather(hidden_one, "mp", axis=3, tiled=True)
    middle = with_halo(gathered, (("seq", 1),), 1)
    deconv_two = upsample(pad_columns(middle), deconv2_weight, 2 * row_count)
    hidden_two = jnp.maximum(deconv_two + deconv2_bias, 0.0).astype(jnp.bfloat16)
    return (
        jnp.dot(
            lax.all_to_all(hidden_two, "mp", split_axis=2, concat_axis=3, tiled=True),
            final_weight,
            preferred_element_type=jnp.float32,
        )
        + final_bias
    ).astype(jnp.bfloat16)

LOG2E = 1.4426950408889634
MIB = 1024 * 1024
NT = (((1,), (1,)), ((), ()))


def dot_nt(left, right):
    return lax.dot_general(left, right, NT, preferred_element_type=jnp.float32)


def whole(shape):
    return pl.BlockSpec(shape, lambda *_: (0,) * len(shape))


def pack_kernel(
    query_ref, keys_ref, values_ref, resid_ref, out_ref, first_ref, last_ref, held_ref, done
):
    copies = []
    for index, source in enumerate((query_ref, keys_ref, values_ref)):
        for row in range(2):
            copy = pltpu.make_async_copy(source.at[0, row], held_ref.at[index, row], done.at[2 * index + row])
            copies.append(copy)
    copies.append(pltpu.make_async_copy(resid_ref.at[0, 0], first_ref, done.at[6]))
    copies.append(pltpu.make_async_copy(resid_ref.at[0, 1], last_ref, done.at[7]))
    for copy in copies:
        copy.start()
    for copy in copies[:6]:
        copy.wait()
    for head in range(out_ref.shape[0] // 2):
        lanes = pl.ds(128 * (head // 2), 128)
        own = slice(64 * (head % 2), 64 * (head % 2) + 64)
        for row in range(2):
            block = out_ref.at[2 * head + row]
            queries, keys, values = (held_ref[index, row, :, lanes][:, own] for index in range(3))
            block[0:32, :] = jnp.concatenate([queries[0:32], queries[32:64]], axis=1)
            block[32:96, :] = jnp.concatenate([keys, values], axis=1)
    for copy in copies[6:]:
        copy.wait()


def pack_tokens(query, keys, values, resid, device_count):
    edge = jax.ShapeDtypeStruct(resid.shape[2:], resid.dtype)
    return pl.pallas_call(
        pack_kernel,
        in_specs=[pl.BlockSpec(memory_space=pl.ANY)] * 4,
        out_shape=(jax.ShapeDtypeStruct((device_count, 96, 128), jnp.bfloat16), edge, edge),
        scratch_shapes=[pltpu.VMEM((3,) + query.shape[1:], jnp.bfloat16), pltpu.SemaphoreType.DMA((8,))],
        compiler_params=pltpu.CompilerParams(vmem_limit_bytes=60 * MIB),
        name="pack_tokens",
    )(query, keys, values, resid)


def reorder_kernel(weight_ref, after_ref, out_ref):
    del after_ref
    out_ref[0] = jnp.swapaxes(weight_ref[:, 0], 0, 1)


def reorder_taps(weight, rows, after):
    channels, _, columns, width = weight.shape
    block = channels // 2 if width > 1024 else channels

    def row_at(place):
        row = rows[0]
        for index in range(1, len(rows)):
            row = jnp.where(place == index, rows[index], row)
        return row

    moved = 2 * len(rows) * channels * columns * width * weight.dtype.itemsize
    return pl.pallas_call(
        reorder_kernel,
        grid=(len(rows), channels // block),
        in_specs=[
            pl.BlockSpec((block, 1, columns, width), lambda i, j: (j, row_at(i), 0, 0)),
            pl.BlockSpec(memory_space=pl.ANY),
        ],
        out_specs=pl.BlockSpec((1, columns, block, width), lambda i, j: (i, 0, j, 0)),
        out_shape=jax.ShapeDtypeStruct((len(rows), columns, channels, width), weight.dtype),
        compiler_params=pltpu.CompilerParams(vmem_limit_bytes=60 * MIB),
        cost_estimate=pl.CostEstimate(flops=0, bytes_accessed=moved, transcendentals=0),
        name="reorder_taps",
    )(weight, after)


def attend_kernel(own_ref, other_ref, out_ref, pairs_ref, values_ref, top_ref, total_ref, mixed_ref, *, sources, chunk):
    half = pairs_ref.shape[0] // 2
    count = 2 * half

    @pl.when(pl.program_id(0) == 0)
    def _():
        pairs_ref[0:half, :] = own_ref[:, 32:96, :].reshape(half, 128)
        pairs_ref[half:count, :] = other_ref[...].reshape(half, 128)
        longest = jnp.zeros((1, 1), jnp.float32)
        for start in range(0, count, 512):
            wide = pairs_ref[start : start + 512, :].astype(jnp.float32).T
            values_ref[:, start : start + 512] = wide[64:128].astype(jnp.bfloat16)
            norms = jnp.sum(wide[0:64] * wide[0:64], axis=0, keepdims=True)
            longest = jnp.maximum(longest, jnp.max(norms, axis=1, keepdims=True))
        top_ref[0:1, 0:128] = jnp.broadcast_to(longest, (1, 128))

    first = pl.program_id(0) * sources
    rows = sources * 32
    packed = own_ref[pl.ds(first, sources), 0:32, :].reshape(rows, 128)
    wide = (packed.astype(jnp.float32) * HEAD_DIM ** (-0.5)).T
    zeros = jnp.zeros((64, rows), jnp.float32)
    exact = jnp.concatenate(
        [jnp.concatenate([wide[0:64], wide[64:128]], axis=1), jnp.concatenate([zeros, zeros], axis=1)], axis=0
    )
    queries = exact.astype(jnp.bfloat16)
    norms = jnp.sum(exact * exact, axis=0, keepdims=True)
    bound = 1.01 * jnp.max(norms * top_ref[0:1, 0:1])
    small = bound <= 50.0 * 50.0

    @pl.when(small)
    def _():
        total, mixed = None, None
        for start in range(0, count, chunk):
            scores = jnp.dot(pairs_ref[start : start + chunk, :], queries, preferred_element_type=jnp.float32)
            exps = jnp.exp2(scores * LOG2E)
            part = jnp.sum(exps, axis=0, keepdims=True)
            product = jnp.dot(
                values_ref[:, start : start + chunk], exps.astype(jnp.bfloat16), preferred_element_type=jnp.float32
            )
            total = part if total is None else total + part
            mixed = product if mixed is None else mixed + product
        total_ref[...] = total
        mixed_ref[...] = mixed

    @pl.when(jnp.logical_not(small))
    def _():
        total_ref[...] = jnp.zeros_like(total_ref)
        mixed_ref[...] = jnp.zeros_like(mixed_ref)

        def absorb(index, top):
            start = pl.multiple_of(index * chunk, chunk)
            scores = jnp.dot(pairs_ref[pl.ds(start, chunk), :], queries, preferred_element_type=jnp.float32)
            fresh = jnp.maximum(top, jnp.max(scores, axis=0, keepdims=True))
            exps = jnp.exp2((scores - fresh) * LOG2E)
            shrink = jnp.exp2((top - fresh) * LOG2E)
            product = jnp.dot(
                values_ref[:, pl.ds(start, chunk)], exps.astype(jnp.bfloat16), preferred_element_type=jnp.float32
            )
            total_ref[...] = total_ref[...] * shrink + jnp.sum(exps, axis=0, keepdims=True)
            mixed_ref[...] = mixed_ref[...] * shrink + product
            return fresh

        lax.fori_loop(0, count // chunk, absorb, jnp.full((1, 2 * rows), -1e30, jnp.float32))

    attended = mixed_ref[...] / total_ref[...]
    joined = jnp.concatenate([attended[:, :rows], attended[:, rows:]], axis=0)
    out_ref[...] = joined.T.astype(jnp.bfloat16).reshape(sources, 32, 128)


def attend(own, other, sources=16, chunk=512):
    count = own.shape[0]
    return pl.pallas_call(
        functools.partial(attend_kernel, sources=sources, chunk=chunk),
        grid=(count // sources,),
        in_specs=[whole(own.shape), whole(other.shape)],
        out_specs=pl.BlockSpec((sources, 32, 128), lambda i: (i, 0, 0)),
        out_shape=jax.ShapeDtypeStruct((count, 32, 128), jnp.bfloat16),
        scratch_shapes=[
            pltpu.VMEM((2 * count * 64, 128), jnp.bfloat16),
            pltpu.VMEM((64, 2 * count * 64), jnp.bfloat16),
            pltpu.VMEM((8, 128), jnp.float32),
            pltpu.VMEM((1, 64 * sources), jnp.float32),
            pltpu.VMEM((64, 64 * sources), jnp.float32),
        ],
        compiler_params=pltpu.CompilerParams(vmem_limit_bytes=40 * MIB),
        name="attend",
    )(own, other)


def shift_columns(field, row_length):
    count = field.shape[0]
    column = lax.broadcasted_iota(jnp.int32, field.shape, 0) % row_length
    before = jnp.where(column == 0, 0.0, pltpu.roll(field, 1, 0))
    after = jnp.where(column == row_length - 1, 0.0, pltpu.roll(field, count - 1, 0))
    return before, after


def store_strided(wide_ref, start, value):
    for group in range(wide_ref.shape[0]):
        lanes = slice(128 * group, 128 * group + 128)
        wide_ref[group, pl.ds(start, value.shape[0], stride=2), :] = value[:, lanes]


def load_wide(wide_ref, rows):
    groups = [wide_ref[group, rows, :] for group in range(wide_ref.shape[0])]
    return jnp.concatenate(groups, axis=1).astype(jnp.bfloat16)


def column_taps(parity):
    return ((1, 1), (0, 3)) if parity == 0 else ((1, 2), (2, 0))


def attended_rows(mixed_ref):
    rows = []
    for parity, which in ((1, 0), (0, 0), (1, 1), (0, 1)):
        low, high = [], []
        for head in range(0, mixed_ref.shape[0], 2):
            left, right = mixed_ref[head, parity, which], mixed_ref[head + 1, parity, which]
            low.append(jnp.concatenate([left[:, :64], right[:, :64]], axis=1))
            high.append(jnp.concatenate([left[:, 64:], right[:, 64:]], axis=1))
        rows += [jnp.concatenate(low, axis=1), jnp.concatenate(high, axis=1)]
    return jnp.concatenate(rows, axis=0)


def head_kernel(
    inside_ref,
    mixed_ref,
    resid_ref,
    above_ref,
    below_ref,
    out_weight_ref,
    gain_ref,
    shift_ref,
    first_taps_ref,
    last_taps_ref,
    bias_one_ref,
    taps_two_ref,
    bias_two_ref,
    final_ref,
    final_bias_ref,
    out_ref,
    projection_ref,
    weight_one_ref,
    weight_two_ref,
    field_ref,
    sums_ref,
    wide_one_ref,
    copies_ref,
    wide_two_ref,
    done,
):
    channels = bias_one_ref.shape[1]
    order = ((1, 0), (1, 1), (3, 0), (3, 1), (2, 0), (2, 1), (0, 0), (0, 1))
    slots = weight_one_ref.shape[0]
    ahead = slots - 1
    first = pltpu.make_async_copy(out_weight_ref, projection_ref, done.at[0])
    last = pltpu.make_async_copy(taps_two_ref, weight_two_ref, done.at[1])
    copies = []
    for index, (_, half) in enumerate(order):
        taps = first_taps_ref.at[index // 2] if index < 6 else last_taps_ref.at[0]
        source = taps.at[pl.ds(2 * half, 2)]
        slot = index % slots
        copies.append(pltpu.make_async_copy(source, weight_one_ref.at[slot], done.at[2 + index]))
    first.start()
    copies[0].start()

    attended = attended_rows(mixed_ref)
    first.wait()
    for copy in copies[1:ahead]:
        copy.start()
    projected = jnp.dot(attended, projection_ref[...], preferred_element_type=jnp.float32)
    for place, resid in enumerate((above_ref[...], resid_ref[0], resid_ref[1], below_ref[...])):
        rows = slice(64 * place, 64 * place + 64)
        stream = resid.astype(jnp.float32) + projected[rows]
        center = jnp.mean(stream, axis=-1, keepdims=True)
        shifted = stream - center
        variance = jnp.mean(shifted * shifted, axis=-1, keepdims=True)
        normed = shifted * lax.rsqrt(variance + EPSILON) * gain_ref[...] + shift_ref[...]
        if place in (0, 3):
            normed = jnp.where(inside_ref[place // 3] > 0, normed, 0.0)
        field_ref[rows, :] = normed.astype(jnp.bfloat16)

    for index, (kernel_row, half) in enumerate(order):
        copies[index].wait()
        if index + ahead < len(order):
            copies[index + ahead].start()
        elif index + ahead == len(order):
            last.start()
        low = 64 if kernel_row < 2 else 0
        weight = weight_one_ref[index % slots].reshape(2 * channels, weight_one_ref.shape[3])
        product = dot_nt(field_ref[low : low + 192, :], weight)
        odd, even = product[:, :channels], product[:, channels:]
        if half == 0:
            odd = shift_columns(odd, 64)[1]
        else:
            even = shift_columns(even, 64)[0]
        if index % 4 == 0:
            sums_ref[0] = even
            sums_ref[1] = odd
        else:
            sums_ref[0] += even
            sums_ref[1] += odd
        if index % 4 == 3:
            for parity in range(2):
                hidden = jnp.maximum(sums_ref[parity] + bias_one_ref[...], 0.0)
                for place in range(3):
                    row = 2 * place + (1 if index == 3 else 0)
                    value = hidden[64 * place : 64 * place + 64]
                    if row in (0, 5):
                        value = jnp.where(inside_ref[row // 5] > 0, value, 0.0)
                    store_strided(wide_one_ref, 128 * row + parity, value)

    hidden = load_wide(wide_one_ref, slice(None))
    before, after = shift_columns(hidden.astype(jnp.float32), 128)
    copies_ref[:, 0:channels] = before.astype(jnp.bfloat16)
    copies_ref[:, channels : 2 * channels] = hidden
    copies_ref[:, 2 * channels :] = after.astype(jnp.bfloat16)
    last.wait()
    for row_parity in range(2):
        for parity in range(2):
            total = None
            for low, kernel_row in (((128, 1), (0, 3)), ((128, 2), (256, 0)))[row_parity]:
                for copy, kernel_col in column_taps(parity):
                    product = dot_nt(
                        copies_ref[low : low + 512, copy * channels : (copy + 1) * channels],
                        weight_two_ref[kernel_row, kernel_col],
                    )
                    total = product if total is None else total + product
            hidden = jnp.maximum(total + bias_two_ref[...], 0.0)
            for place in range(4):
                start = 256 * (2 * place + row_parity) + parity
                store_strided(wide_two_ref, start, hidden[128 * place : 128 * place + 128])
    for row in range(8):
        hidden = load_wide(wide_two_ref, slice(256 * row, 256 * row + 256))
        heat = dot_nt(final_ref[...], hidden) + final_bias_ref[...]
        out_ref[row] = heat.astype(jnp.bfloat16)


def keypoint_head(
    inside,
    mixed,
    resid,
    above,
    below,
    out_weight,
    gain,
    shift,
    first_taps,
    last_taps,
    bias_one,
    taps_two,
    bias_two,
    final_weight,
    final_bias,
):
    width = resid.shape[-1]
    channels = bias_one.shape[0]
    keypoints = final_weight.shape[1]
    near = pl.BlockSpec(memory_space=pltpu.VMEM)
    far = pl.BlockSpec(memory_space=pl.ANY)
    return pl.pallas_call(
        head_kernel,
        in_specs=[pl.BlockSpec(memory_space=pltpu.SMEM), near, near, near, near, far, near, near]
        + [far, far, near, far, near, near, near],
        out_shape=jax.ShapeDtypeStruct((8, keypoints, 256), jnp.bfloat16),
        scratch_shapes=[
            pltpu.VMEM(out_weight.shape, jnp.bfloat16),
            pltpu.VMEM((5, 2, channels, width), jnp.bfloat16),
            pltpu.VMEM((4, 4, channels, channels), jnp.bfloat16),
            pltpu.VMEM((256, width), jnp.bfloat16),
            pltpu.VMEM((2, 192, channels), jnp.float32),
            pltpu.VMEM((channels // 128, 768, 128), jnp.float32),
            pltpu.VMEM((768, 3 * channels), jnp.bfloat16),
            pltpu.VMEM((channels // 128, 2048, 128), jnp.float32),
            pltpu.SemaphoreType.DMA((10,)),
        ],
        compiler_params=pltpu.CompilerParams(vmem_limit_bytes=57 * MIB + MIB // 2),
        name="keypoint_head",
    )(
        inside,
        mixed,
        resid,
        above,
        below,
        out_weight,
        gain.reshape(1, -1),
        shift.reshape(1, -1),
        first_taps,
        last_taps,
        bias_one.reshape(1, -1),
        taps_two,
        bias_two.reshape(1, -1),
        final_weight.T,
        final_bias.reshape(-1, 1),
    )


def by_heads(
    query,
    keys,
    values,
    resid,
    out_weight,
    norm_gain,
    norm_bias,
    deconv1_weight,
    deconv1_bias,
    deconv2_weight,
    deconv2_bias,
    final_weight,
    final_bias,
):
    count = lax.axis_size("seq")
    place = lax.axis_index("seq")
    up = [(i, i + 1) for i in range(count - 1)]
    down = [(i + 1, i) for i in range(count - 1)]
    swap = [(i, i ^ 1) for i in range(count)]

    packed, first_row, last_row = pack_tokens(query, keys, values, resid, count)
    own = lax.all_to_all(packed, "seq", 0, 0, tiled=True)
    above = lax.ppermute(last_row, "seq", up)
    below = lax.ppermute(first_row, "seq", down)
    first_taps = reorder_taps(deconv1_weight, (1, 3, 2), packed)
    own, above, below, first_taps = lax.optimization_barrier((own, above, below, first_taps))
    other = lax.ppermute(own[:, 32:96], "seq", swap)
    mixed = attend(own, other)
    last_taps = reorder_taps(deconv1_weight, (0,), mixed)
    taps_two = reorder_taps(deconv2_weight, (0, 1, 2, 3), mixed)

    rim = jnp.zeros((1, 32, 128), jnp.bfloat16)
    earlier = jnp.concatenate([rim, mixed[:-1]], axis=0)
    later = jnp.concatenate([mixed[1:], rim], axis=0)
    odd = place % 2 == 1
    sent = jnp.stack([jnp.where(odd, earlier, mixed), jnp.where(odd, mixed, later)], axis=1)
    back = lax.all_to_all(sent, "seq", 0, 0, tiled=True)
    back = back.reshape(count // 2, 2, 2, 32, 128)

    inside = jnp.stack([place > 0, place < count - 1]).astype(jnp.int32)
    heat = keypoint_head(
        inside,
        back,
        resid[0],
        above,
        below,
        out_weight,
        norm_gain,
        norm_bias,
        first_taps,
        last_taps,
        deconv1_bias,
        taps_two,
        deconv2_bias,
        final_weight,
        final_bias,
    )
    return jnp.transpose(heat, (0, 2, 1))[None]


def step(*arrays):
    query = arrays[0]
    frames, rows, columns, width = query.shape
    heads = width // HEAD_DIM
    whole_heads = lax.axis_size("mp") == 1 and lax.axis_size("seq") == 2 * heads
    if whole_heads and (frames, rows, columns) == (1, 2, 64):
        return by_heads(*arrays)
    return local(*arrays)


def solution(mesh):
    placed = (
        P(None, "seq", None, "mp"),
        P(None, "seq", None, "mp"),
        P(None, "seq", None, "mp"),
        P(None, "seq", "mp", None),
        P("mp", None),
        P(),
        P(),
        P("mp", None, None, None),
        P("mp"),
        P("mp", None, None, None),
        P("mp"),
        P(),
        P(),
    )
    return jax.shard_map(
        step, mesh=mesh, in_specs=placed, out_specs=P(None, "seq", "mp", None), check_vma=False
    )
```

```python
import functools

import jax
import jax.numpy as jnp
from jax import lax
from jax.experimental import pallas as pl
from jax.experimental.pallas import tpu as pltpu
from jax.sharding import PartitionSpec as P

HEAD_DIM = 64


TAP_TABLE = (((1, 1), (0, 3)), ((2, 0), (1, 2)))
EPSILON = 1e-06


def with_halo(array, sides, width):
    for axis, dim in sides:
        size, length = (lax.axis_size(axis), array.shape[dim])
        up = [(i, (i + 1) % size) for i in range(size - 1)]
        down = [(j, i) for i, j in up]
        last = lax.slice_in_dim(array, length - width, length, axis=dim)
        first = lax.slice_in_dim(array, 0, width, axis=dim)
        before = lax.ppermute(last, axis, up)
        after = lax.ppermute(first, axis, down)
        array = jnp.concatenate([before, array, after], axis=dim)
    return array


def tap_product(window, weight, kernel_row, kernel_col):
    tap = weight[:, kernel_row, kernel_col, :]
    return lax.dot_general(
        window, tap, (((3,), (1,)), ((), ())), preferred_element_type=jnp.float32
    )


def half_rows(padded, weight, tap_pairs, first_row, row_count):
    col_count = padded.shape[2] - 2
    halves = []
    for col_parity in range(2):
        summed = None
        for pad_row, kernel_row in tap_pairs:
            for pad_col, kernel_col in TAP_TABLE[col_parity]:
                window = padded[
                    :,
                    first_row + pad_row : first_row + pad_row + row_count,
                    pad_col : pad_col + col_count,
                    :,
                ]
                product = tap_product(window, weight, kernel_row, kernel_col)
                summed = product if summed is None else summed + product
        halves.append(summed)
    stacked = jnp.stack(halves, axis=3)
    return stacked.reshape(stacked.shape[0], row_count, 2 * col_count, stacked.shape[-1])


def upsample(padded, weight, row_count):
    even_rows = half_rows(padded, weight, TAP_TABLE[0], 0, row_count)
    odd_rows = half_rows(padded, weight, TAP_TABLE[1], 0, row_count)
    stacked = jnp.stack([even_rows, odd_rows], axis=2)
    return stacked.reshape(stacked.shape[0], 2 * row_count, stacked.shape[3], stacked.shape[4])


def pad_columns(field):
    return jnp.pad(field, ((0, 0), (0, 0), (1, 1), (0, 0)))


def layer_norm(stream, norm_gain, norm_bias):
    center = jnp.mean(stream, axis=-1, keepdims=True)
    shifted = stream - center
    variance = jnp.mean(shifted * shifted, axis=-1, keepdims=True)
    return (shifted * lax.rsqrt(variance + EPSILON) * norm_gain + norm_bias).astype(jnp.bfloat16)


def local(
    query,
    keys,
    values,
    resid,
    out_weight,
    norm_gain,
    norm_bias,
    deconv1_weight,
    deconv1_bias,
    deconv2_weight,
    deconv2_bias,
    final_weight,
    final_bias,
):
    frame_count, row_count, col_count, feature_width = query.shape
    local_heads = feature_width // HEAD_DIM
    score_scale = HEAD_DIM ** (-0.5)
    query_count = row_count * col_count
    queries = query.reshape(frame_count, query_count, local_heads, HEAD_DIM)
    start_max = jnp.full((frame_count, query_count, local_heads), -1e30, jnp.float32)
    running_max = start_max
    key_piece = lax.all_gather(keys, "seq", axis=1, tiled=True).reshape(
        frame_count, -1, local_heads, HEAD_DIM
    )
    value_piece = lax.all_gather(values, "seq", axis=1, tiled=True).reshape(
        frame_count, -1, local_heads, HEAD_DIM
    )
    scores = (
        jnp.einsum("fqhd,fkhd->fqhk", queries, key_piece, preferred_element_type=jnp.float32)
        * score_scale
    )
    fresh_max = jnp.maximum(running_max, jnp.max(scores, axis=-1))
    exps = jnp.exp(scores - fresh_max[..., None])
    denominator = jnp.sum(exps, axis=-1)
    weighted = jnp.einsum(
        "fqhk,fkhd->fqhd",
        exps.astype(jnp.bfloat16),
        value_piece,
        preferred_element_type=jnp.float32,
    )
    running_max, denominator, weighted = (fresh_max, denominator, weighted)
    attended = (
        (weighted / denominator[..., None])
        .astype(jnp.bfloat16)
        .reshape(frame_count, row_count, col_count, feature_width)
    )
    partial_value = jnp.dot(attended, out_weight, preferred_element_type=jnp.float32)
    summed = lax.psum(partial_value.astype(jnp.bfloat16), "mp").astype(jnp.float32)
    full_resid = lax.all_gather(resid, "mp", axis=2, tiled=True)
    normed = layer_norm(full_resid.astype(jnp.float32) + summed, norm_gain, norm_bias)
    rimmed = with_halo(normed, (("seq", 1),), 1)
    padded = pad_columns(rimmed)
    deconv_one = upsample(padded, deconv1_weight, row_count)
    hidden_one = jnp.maximum(deconv_one + deconv1_bias, 0.0).astype(jnp.bfloat16)
    gathered = lax.all_gather(hidden_one, "mp", axis=3, tiled=True)
    middle = with_halo(gathered, (("seq", 1),), 1)
    deconv_two = upsample(pad_columns(middle), deconv2_weight, 2 * row_count)
    hidden_two = jnp.maximum(deconv_two + deconv2_bias, 0.0).astype(jnp.bfloat16)
    return (
        jnp.dot(
            lax.all_to_all(hidden_two, "mp", split_axis=2, concat_axis=3, tiled=True),
            final_weight,
            preferred_element_type=jnp.float32,
        )
        + final_bias
    ).astype(jnp.bfloat16)

LOG2E = 1.4426950408889634
MIB = 1024 * 1024
NT = (((1,), (1,)), ((), ()))


def dot_nt(left, right):
    return lax.dot_general(left, right, NT, preferred_element_type=jnp.float32)


def whole(shape):
    return pl.BlockSpec(shape, lambda *_: (0,) * len(shape))


def pack_kernel(
    query_ref, keys_ref, values_ref, resid_ref, out_ref, first_ref, last_ref, held_ref, done
):
    copies = []
    for index, source in enumerate((query_ref, keys_ref, values_ref)):
        for row in range(2):
            copy = pltpu.make_async_copy(source.at[0, row], held_ref.at[index, row], done.at[2 * index + row])
            copies.append(copy)
    copies.append(pltpu.make_async_copy(resid_ref.at[0, 0], first_ref, done.at[6]))
    copies.append(pltpu.make_async_copy(resid_ref.at[0, 1], last_ref, done.at[7]))
    for copy in copies:
        copy.start()
    for copy in copies[:6]:
        copy.wait()
    for head in range(out_ref.shape[0] // 2):
        lanes = pl.ds(128 * (head // 2), 128)
        own = slice(64 * (head % 2), 64 * (head % 2) + 64)
        for row in range(2):
            block = out_ref.at[2 * head + row]
            queries, keys, values = (held_ref[index, row, :, lanes][:, own] for index in range(3))
            block[0:32, :] = jnp.concatenate([queries[0:32], queries[32:64]], axis=1)
            block[32:96, :] = jnp.concatenate([keys, values], axis=1)
    for copy in copies[6:]:
        copy.wait()


def pack_tokens(query, keys, values, resid, device_count):
    edge = jax.ShapeDtypeStruct(resid.shape[2:], resid.dtype)
    return pl.pallas_call(
        pack_kernel,
        in_specs=[pl.BlockSpec(memory_space=pl.ANY)] * 4,
        out_shape=(jax.ShapeDtypeStruct((device_count, 96, 128), jnp.bfloat16), edge, edge),
        scratch_shapes=[pltpu.VMEM((3,) + query.shape[1:], jnp.bfloat16), pltpu.SemaphoreType.DMA((8,))],
        compiler_params=pltpu.CompilerParams(vmem_limit_bytes=60 * MIB),
        name="pack_tokens",
    )(query, keys, values, resid)


def reorder_kernel(weight_ref, after_ref, out_ref):
    del after_ref
    out_ref[0] = jnp.swapaxes(weight_ref[:, 0], 0, 1)


def reorder_taps(weight, rows, after):
    channels, _, columns, width = weight.shape
    block = channels // 2 if width > 1024 else channels

    def row_at(place):
        row = rows[0]
        for index in range(1, len(rows)):
            row = jnp.where(place == index, rows[index], row)
        return row

    moved = 2 * len(rows) * channels * columns * width * weight.dtype.itemsize
    return pl.pallas_call(
        reorder_kernel,
        grid=(len(rows), channels // block),
        in_specs=[
            pl.BlockSpec((block, 1, columns, width), lambda i, j: (j, row_at(i), 0, 0)),
            pl.BlockSpec(memory_space=pl.ANY),
        ],
        out_specs=pl.BlockSpec((1, columns, block, width), lambda i, j: (i, 0, j, 0)),
        out_shape=jax.ShapeDtypeStruct((len(rows), columns, channels, width), weight.dtype),
        compiler_params=pltpu.CompilerParams(vmem_limit_bytes=60 * MIB),
        cost_estimate=pl.CostEstimate(flops=0, bytes_accessed=moved, transcendentals=0),
        name="reorder_taps",
    )(weight, after)


def pair_kernel(weight_ref, after_ref, out_ref):
    del after_ref
    width = weight_ref.shape[3]
    taps = jnp.swapaxes(weight_ref[:, 0], 0, 1)
    for parity, columns in enumerate(((3, 1), (2, 0))):
        for place, column in enumerate(columns):
            out_ref[0, parity, :, place * width : (place + 1) * width] = taps[column]


def pair_taps(weight, after):
    channels, rows, columns, width = weight.shape
    moved = 2 * channels * rows * columns * width * weight.dtype.itemsize
    return pl.pallas_call(
        pair_kernel,
        grid=(rows,),
        in_specs=[
            pl.BlockSpec((channels, 1, columns, width), lambda i: (0, i, 0, 0)),
            pl.BlockSpec(memory_space=pl.ANY),
        ],
        out_specs=pl.BlockSpec((1, 2, channels, 2 * width), lambda i: (i, 0, 0, 0)),
        out_shape=jax.ShapeDtypeStruct((rows, 2, channels, 2 * width), weight.dtype),
        compiler_params=pltpu.CompilerParams(vmem_limit_bytes=60 * MIB),
        cost_estimate=pl.CostEstimate(flops=0, bytes_accessed=moved, transcendentals=0),
        name="pair_taps",
    )(weight, after)


def attend_kernel(parity_ref, own_ref, other_ref, out_ref, pairs_ref, values_ref, top_ref, total_ref, mixed_ref, *, sources, chunk):
    half = pairs_ref.shape[0] // 2
    count = 2 * half

    @pl.when(pl.program_id(0) == 0)
    def _():
        pairs_ref[0:half, :] = own_ref[:, 32:96, :].reshape(half, 128)
        pairs_ref[half:count, :] = other_ref[...].reshape(half, 128)
        longest = jnp.zeros((1, 1), jnp.float32)
        for start in range(0, count, 512):
            wide = pairs_ref[start : start + 512, :].astype(jnp.float32).T
            values_ref[:, start : start + 512] = wide[64:128].astype(jnp.bfloat16)
            norms = jnp.sum(wide[0:64] * wide[0:64], axis=0, keepdims=True)
            longest = jnp.maximum(longest, jnp.max(norms, axis=1, keepdims=True))
        top_ref[0:1, 0:128] = jnp.broadcast_to(longest, (1, 128))

    first = pl.program_id(0) * sources
    rows = sources * 32
    packed = own_ref[pl.ds(first, sources), 0:32, :].reshape(rows, 128)
    wide = (packed.astype(jnp.float32) * HEAD_DIM ** (-0.5)).T
    zeros = jnp.zeros((64, rows), jnp.float32)
    exact = jnp.concatenate(
        [jnp.concatenate([wide[0:64], wide[64:128]], axis=1), jnp.concatenate([zeros, zeros], axis=1)], axis=0
    )
    queries = exact.astype(jnp.bfloat16)
    norms = jnp.sum(exact * exact, axis=0, keepdims=True)
    bound = 1.01 * jnp.max(norms * top_ref[0:1, 0:1])
    small = bound <= 50.0 * 50.0

    @pl.when(small)
    def _():
        total, mixed = None, None
        for start in range(0, count, chunk):
            scores = jnp.dot(pairs_ref[start : start + chunk, :], queries, preferred_element_type=jnp.float32)
            exps = jnp.exp2(scores * LOG2E)
            part = jnp.sum(exps, axis=0, keepdims=True)
            product = jnp.dot(
                values_ref[:, start : start + chunk], exps.astype(jnp.bfloat16), preferred_element_type=jnp.float32
            )
            total = part if total is None else total + part
            mixed = product if mixed is None else mixed + product
        total_ref[...] = total
        mixed_ref[...] = mixed

    @pl.when(jnp.logical_not(small))
    def _():
        total_ref[...] = jnp.zeros_like(total_ref)
        mixed_ref[...] = jnp.zeros_like(mixed_ref)

        def absorb(index, top):
            start = pl.multiple_of(index * chunk, chunk)
            scores = jnp.dot(pairs_ref[pl.ds(start, chunk), :], queries, preferred_element_type=jnp.float32)
            fresh = jnp.maximum(top, jnp.max(scores, axis=0, keepdims=True))
            exps = jnp.exp2((scores - fresh) * LOG2E)
            shrink = jnp.exp2((top - fresh) * LOG2E)
            product = jnp.dot(
                values_ref[:, pl.ds(start, chunk)], exps.astype(jnp.bfloat16), preferred_element_type=jnp.float32
            )
            total_ref[...] = total_ref[...] * shrink + jnp.sum(exps, axis=0, keepdims=True)
            mixed_ref[...] = mixed_ref[...] * shrink + product
            return fresh

        lax.fori_loop(0, count // chunk, absorb, jnp.full((1, 2 * rows), -1e30, jnp.float32))

    attended = mixed_ref[...] / total_ref[...]
    joined = jnp.concatenate([attended[:, :rows], attended[:, rows:]], axis=0)
    rows = joined.T.astype(jnp.bfloat16).reshape(sources, 32, 128)
    steps = out_ref.shape[0] // sources
    rim = jnp.zeros((32, 128), jnp.bfloat16)
    for step in range(steps):
        start, stop = step * sources, (step + 1) * sources

        @pl.when((pl.program_id(0) == step) & (parity_ref[0] == 0))
        def _():
            out_ref[start:stop, 0] = rows
            if step == 0:
                out_ref[0 : stop - 1, 1] = rows[1:]
                out_ref[steps * sources - 1, 1] = rim
            else:
                out_ref[start - 1 : stop - 1, 1] = rows

        @pl.when((pl.program_id(0) == step) & (parity_ref[0] == 1))
        def _():
            out_ref[start:stop, 1] = rows
            if step == 0:
                out_ref[0, 0] = rim
            if step == steps - 1:
                out_ref[start + 1 : stop, 0] = rows[:-1]
            else:
                out_ref[start + 1 : stop + 1, 0] = rows


def attend(parity, own, other, sources=16, chunk=512):
    count = own.shape[0]
    return pl.pallas_call(
        functools.partial(attend_kernel, sources=sources, chunk=chunk),
        grid=(count // sources,),
        in_specs=[pl.BlockSpec(memory_space=pltpu.SMEM), whole(own.shape), whole(other.shape)],
        out_specs=whole((count, 2, 32, 128)),
        out_shape=jax.ShapeDtypeStruct((count, 2, 32, 128), jnp.bfloat16),
        scratch_shapes=[
            pltpu.VMEM((2 * count * 64, 128), jnp.bfloat16),
            pltpu.VMEM((64, 2 * count * 64), jnp.bfloat16),
            pltpu.VMEM((8, 128), jnp.float32),
            pltpu.VMEM((1, 64 * sources), jnp.float32),
            pltpu.VMEM((64, 64 * sources), jnp.float32),
        ],
        compiler_params=pltpu.CompilerParams(vmem_limit_bytes=40 * MIB),
        name="attend",
    )(parity, own, other)


def shift_columns(field, row_length):
    count = field.shape[0]
    column = lax.broadcasted_iota(jnp.int32, field.shape, 0) % row_length
    before = jnp.where(column == 0, 0.0, pltpu.roll(field, 1, 0))
    after = jnp.where(column == row_length - 1, 0.0, pltpu.roll(field, count - 1, 0))
    return before, after


def store_strided(wide_ref, start, value):
    for group in range(wide_ref.shape[0]):
        lanes = slice(128 * group, 128 * group + 128)
        wide_ref[group, pl.ds(start, value.shape[0], stride=2), :] = value[:, lanes]


def load_wide(wide_ref, rows):
    groups = [wide_ref[group, rows, :] for group in range(wide_ref.shape[0])]
    return jnp.concatenate(groups, axis=1).astype(jnp.bfloat16)


def attended_rows(mixed_ref):
    rows = []
    for parity, which in ((1, 0), (0, 0), (1, 1), (0, 1)):
        low, high = [], []
        for head in range(0, mixed_ref.shape[0], 2):
            left, right = mixed_ref[head, parity, which], mixed_ref[head + 1, parity, which]
            low.append(jnp.concatenate([left[:, :64], right[:, :64]], axis=1))
            high.append(jnp.concatenate([left[:, 64:], right[:, 64:]], axis=1))
        rows += [jnp.concatenate(low, axis=1), jnp.concatenate(high, axis=1)]
    return jnp.concatenate(rows, axis=0)


def head_kernel(
    inside_ref,
    mixed_ref,
    resid_ref,
    above_ref,
    below_ref,
    out_weight_ref,
    gain_ref,
    shift_ref,
    first_taps_ref,
    last_taps_ref,
    bias_one_ref,
    taps_two_ref,
    bias_two_ref,
    final_ref,
    final_bias_ref,
    out_ref,
    projection_ref,
    weight_one_ref,
    weight_two_ref,
    field_ref,
    sums_ref,
    wide_one_ref,
    copies_ref,
    wide_two_ref,
    heat_ref,
    done,
):
    channels = bias_one_ref.shape[0]
    slots = weight_one_ref.shape[0]
    ahead = slots - 1
    first = pltpu.make_async_copy(out_weight_ref, projection_ref, done.at[0])
    last = pltpu.make_async_copy(taps_two_ref, weight_two_ref, done.at[1])
    copies = []
    for index in range(4):
        source = first_taps_ref.at[index] if index < 3 else last_taps_ref.at[0]
        slot = index % slots
        copies.append(pltpu.make_async_copy(source, weight_one_ref.at[slot], done.at[2 + index]))
    first.start()
    copies[0].start()

    attended = attended_rows(mixed_ref)
    first.wait()
    for copy in copies[1:]:
        copy.start()
    last.start()
    projected = jnp.dot(attended, projection_ref[...], preferred_element_type=jnp.float32)
    for place, resid in enumerate((above_ref[...], resid_ref[0], resid_ref[1], below_ref[...])):
        rows = slice(64 * place, 64 * place + 64)
        stream = resid.astype(jnp.float32) + projected[rows]
        center = jnp.mean(stream, axis=-1, keepdims=True)
        shifted = stream - center
        variance = jnp.mean(shifted * shifted, axis=-1, keepdims=True)
        normed = shifted * lax.rsqrt(variance + EPSILON) * gain_ref[...][None, :] + shift_ref[...][None, :]
        if place in (0, 3):
            normed = jnp.where(inside_ref[place // 3] > 0, normed, 0.0)
        field_ref[rows, :] = normed.astype(jnp.bfloat16)

    for index, kernel_row in enumerate((1, 3, 2, 0)):
        copies[index].wait()
        if index == 3:
            last.wait()
        low = 64 if kernel_row < 2 else 0
        weight = weight_one_ref[index % slots].reshape(4 * channels, weight_one_ref.shape[3])
        product = dot_nt(field_ref[low : low + 192, :], weight)
        parts = [product[:, channels * column : channels * (column + 1)] for column in range(4)]
        odd = shift_columns(parts[0], 64)[1] + parts[2]
        even = shift_columns(parts[3], 64)[0] + parts[1]
        if index % 2 == 0:
            sums_ref[0] = even
            sums_ref[1] = odd
        else:
            for parity in range(2):
                hidden = jnp.maximum((even, odd)[parity] + sums_ref[parity] + bias_one_ref[...][None, :], 0.0)
                for place in range(3):
                    row = 2 * place + (1 if index == 1 else 0)
                    value = hidden[64 * place : 64 * place + 64]
                    if row in (0, 5):
                        value = jnp.where(inside_ref[row // 5] > 0, value, 0.0)
                    store_strided(wide_one_ref, 128 * row + parity, value)

    hidden = load_wide(wide_one_ref, slice(None))
    before, after = shift_columns(hidden.astype(jnp.float32), 128)
    copies_ref[:, 0:channels] = before.astype(jnp.bfloat16)
    copies_ref[:, channels : 2 * channels] = hidden
    copies_ref[:, 2 * channels :] = after.astype(jnp.bfloat16)
    for row_parity in range(2):
        for parity in range(2):
            total = None
            lanes = slice(parity * channels, (parity + 2) * channels)
            for low, kernel_row in (((128, 1), (0, 3)), ((128, 2), (256, 0)))[row_parity]:
                product = dot_nt(copies_ref[low : low + 512, lanes], weight_two_ref[kernel_row, parity])
                total = product if total is None else total + product
            hidden = jnp.maximum(total + bias_two_ref[...][None, :], 0.0)
            for place in range(4):
                start = 256 * (2 * place + row_parity) + parity
                store_strided(wide_two_ref, start, hidden[128 * place : 128 * place + 128])
    for row in range(8):
        hidden = load_wide(wide_two_ref, slice(256 * row, 256 * row + 256))
        heat = dot_nt(final_ref[...], hidden) + final_bias_ref[...]
        heat_ref[row] = heat.astype(jnp.bfloat16)
    out_ref[...] = jnp.swapaxes(heat_ref[...], 0, 1)


def keypoint_head(
    inside,
    mixed,
    resid,
    above,
    below,
    out_weight,
    gain,
    shift,
    first_taps,
    last_taps,
    bias_one,
    taps_two,
    bias_two,
    final_weight,
    final_bias,
):
    width = resid.shape[-1]
    channels = bias_one.shape[0]
    keypoints = final_weight.shape[1]
    near = pl.BlockSpec(memory_space=pltpu.VMEM)
    far = pl.BlockSpec(memory_space=pl.ANY)
    return pl.pallas_call(
        head_kernel,
        in_specs=[pl.BlockSpec(memory_space=pltpu.SMEM), near, near, near, near, far, near, near]
        + [far, far, near, far, near, near, near],
        out_shape=jax.ShapeDtypeStruct((keypoints, 8, 256), jnp.bfloat16),
        scratch_shapes=[
            pltpu.VMEM(out_weight.shape, jnp.bfloat16),
            pltpu.VMEM((4, 4, channels, width), jnp.bfloat16),
            pltpu.VMEM((4, 2, channels, 2 * channels), jnp.bfloat16),
            pltpu.VMEM((256, width), jnp.bfloat16),
            pltpu.VMEM((2, 192, channels), jnp.float32),
            pltpu.VMEM((channels // 128, 768, 128), jnp.float32),
            pltpu.VMEM((768, 3 * channels), jnp.bfloat16),
            pltpu.VMEM((channels // 128, 2048, 128), jnp.float32),
            pltpu.VMEM((8, keypoints, 256), jnp.bfloat16),
            pltpu.SemaphoreType.DMA((6,)),
        ],
        compiler_params=pltpu.CompilerParams(vmem_limit_bytes=57 * MIB + MIB // 2),
        name="keypoint_head",
    )(
        inside,
        mixed,
        resid,
        above,
        below,
        out_weight,
        gain,
        shift,
        first_taps,
        last_taps,
        bias_one,
        taps_two,
        bias_two,
        final_weight.T,
        final_bias.reshape(-1, 1),
    )


def by_heads(
    query,
    keys,
    values,
    resid,
    out_weight,
    norm_gain,
    norm_bias,
    deconv1_weight,
    deconv1_bias,
    deconv2_weight,
    deconv2_bias,
    final_weight,
    final_bias,
):
    count = lax.axis_size("seq")
    place = lax.axis_index("seq")
    up = [(i, i + 1) for i in range(count - 1)]
    down = [(i + 1, i) for i in range(count - 1)]
    swap = [(i, i ^ 1) for i in range(count)]

    packed, first_row, last_row = pack_tokens(query, keys, values, resid, count)
    own = lax.all_to_all(packed, "seq", 0, 0, tiled=True)
    above = lax.ppermute(last_row, "seq", up)
    below = lax.ppermute(first_row, "seq", down)
    first_taps = reorder_taps(deconv1_weight, (1, 3, 2), packed)
    own, above, below, first_taps = lax.optimization_barrier((own, above, below, first_taps))
    other = lax.ppermute(own[:, 32:96], "seq", swap)
    sent = attend((place % 2).astype(jnp.int32).reshape(1), own, other)
    last_taps = reorder_taps(deconv1_weight, (0,), sent)
    taps_two = pair_taps(deconv2_weight, sent)
    back = lax.all_to_all(sent, "seq", 0, 0, tiled=True)
    back = back.reshape(count // 2, 2, 2, 32, 128)

    inside = jnp.stack([place > 0, place < count - 1]).astype(jnp.int32)
    heat = keypoint_head(
        inside,
        back,
        resid[0],
        above,
        below,
        out_weight,
        norm_gain,
        norm_bias,
        first_taps,
        last_taps,
        deconv1_bias,
        taps_two,
        deconv2_bias,
        final_weight,
        final_bias,
    )
    return jnp.transpose(heat, (1, 2, 0))[None]


def step(*arrays):
    query = arrays[0]
    frames, rows, columns, width = query.shape
    heads = width // HEAD_DIM
    whole_heads = lax.axis_size("mp") == 1 and lax.axis_size("seq") == 2 * heads
    if whole_heads and (frames, rows, columns) == (1, 2, 64):
        return by_heads(*arrays)
    return local(*arrays)


def solution(mesh):
    placed = (
        P(None, "seq", None, "mp"),
        P(None, "seq", None, "mp"),
        P(None, "seq", None, "mp"),
        P(None, "seq", "mp", None),
        P("mp", None),
        P(),
        P(),
        P("mp", None, None, None),
        P("mp"),
        P("mp", None, None, None),
        P("mp"),
        P(),
        P(),
    )
    return jax.shard_map(
        step, mesh=mesh, in_specs=placed, out_specs=P(None, "seq", "mp", None), check_vma=False
    )
```

```python
import functools

import jax
import jax.numpy as jnp
from jax import lax
from jax.experimental import pallas as pl
from jax.experimental.pallas import tpu as pltpu
from jax.sharding import PartitionSpec as P

HEAD_DIM = 64


TAP_TABLE = (((1, 1), (0, 3)), ((2, 0), (1, 2)))
EPSILON = 1e-06


def with_halo(array, sides, width):
    for axis, dim in sides:
        size, length = (lax.axis_size(axis), array.shape[dim])
        up = [(i, (i + 1) % size) for i in range(size - 1)]
        down = [(j, i) for i, j in up]
        last = lax.slice_in_dim(array, length - width, length, axis=dim)
        first = lax.slice_in_dim(array, 0, width, axis=dim)
        before = lax.ppermute(last, axis, up)
        after = lax.ppermute(first, axis, down)
        array = jnp.concatenate([before, array, after], axis=dim)
    return array


def tap_product(window, weight, kernel_row, kernel_col):
    tap = weight[:, kernel_row, kernel_col, :]
    return lax.dot_general(
        window, tap, (((3,), (1,)), ((), ())), preferred_element_type=jnp.float32
    )


def half_rows(padded, weight, tap_pairs, first_row, row_count):
    col_count = padded.shape[2] - 2
    halves = []
    for col_parity in range(2):
        summed = None
        for pad_row, kernel_row in tap_pairs:
            for pad_col, kernel_col in TAP_TABLE[col_parity]:
                window = padded[
                    :,
                    first_row + pad_row : first_row + pad_row + row_count,
                    pad_col : pad_col + col_count,
                    :,
                ]
                product = tap_product(window, weight, kernel_row, kernel_col)
                summed = product if summed is None else summed + product
        halves.append(summed)
    stacked = jnp.stack(halves, axis=3)
    return stacked.reshape(stacked.shape[0], row_count, 2 * col_count, stacked.shape[-1])


def upsample(padded, weight, row_count):
    even_rows = half_rows(padded, weight, TAP_TABLE[0], 0, row_count)
    odd_rows = half_rows(padded, weight, TAP_TABLE[1], 0, row_count)
    stacked = jnp.stack([even_rows, odd_rows], axis=2)
    return stacked.reshape(stacked.shape[0], 2 * row_count, stacked.shape[3], stacked.shape[4])


def pad_columns(field):
    return jnp.pad(field, ((0, 0), (0, 0), (1, 1), (0, 0)))


def layer_norm(stream, norm_gain, norm_bias):
    center = jnp.mean(stream, axis=-1, keepdims=True)
    shifted = stream - center
    variance = jnp.mean(shifted * shifted, axis=-1, keepdims=True)
    return (shifted * lax.rsqrt(variance + EPSILON) * norm_gain + norm_bias).astype(jnp.bfloat16)


def local(
    query,
    keys,
    values,
    resid,
    out_weight,
    norm_gain,
    norm_bias,
    deconv1_weight,
    deconv1_bias,
    deconv2_weight,
    deconv2_bias,
    final_weight,
    final_bias,
):
    frame_count, row_count, col_count, feature_width = query.shape
    local_heads = feature_width // HEAD_DIM
    score_scale = HEAD_DIM ** (-0.5)
    query_count = row_count * col_count
    queries = query.reshape(frame_count, query_count, local_heads, HEAD_DIM)
    start_max = jnp.full((frame_count, query_count, local_heads), -1e30, jnp.float32)
    running_max = start_max
    key_piece = lax.all_gather(keys, "seq", axis=1, tiled=True).reshape(
        frame_count, -1, local_heads, HEAD_DIM
    )
    value_piece = lax.all_gather(values, "seq", axis=1, tiled=True).reshape(
        frame_count, -1, local_heads, HEAD_DIM
    )
    scores = (
        jnp.einsum("fqhd,fkhd->fqhk", queries, key_piece, preferred_element_type=jnp.float32)
        * score_scale
    )
    fresh_max = jnp.maximum(running_max, jnp.max(scores, axis=-1))
    exps = jnp.exp(scores - fresh_max[..., None])
    denominator = jnp.sum(exps, axis=-1)
    weighted = jnp.einsum(
        "fqhk,fkhd->fqhd",
        exps.astype(jnp.bfloat16),
        value_piece,
        preferred_element_type=jnp.float32,
    )
    running_max, denominator, weighted = (fresh_max, denominator, weighted)
    attended = (
        (weighted / denominator[..., None])
        .astype(jnp.bfloat16)
        .reshape(frame_count, row_count, col_count, feature_width)
    )
    partial_value = jnp.dot(attended, out_weight, preferred_element_type=jnp.float32)
    summed = lax.psum(partial_value.astype(jnp.bfloat16), "mp").astype(jnp.float32)
    full_resid = lax.all_gather(resid, "mp", axis=2, tiled=True)
    normed = layer_norm(full_resid.astype(jnp.float32) + summed, norm_gain, norm_bias)
    rimmed = with_halo(normed, (("seq", 1),), 1)
    padded = pad_columns(rimmed)
    deconv_one = upsample(padded, deconv1_weight, row_count)
    hidden_one = jnp.maximum(deconv_one + deconv1_bias, 0.0).astype(jnp.bfloat16)
    gathered = lax.all_gather(hidden_one, "mp", axis=3, tiled=True)
    middle = with_halo(gathered, (("seq", 1),), 1)
    deconv_two = upsample(pad_columns(middle), deconv2_weight, 2 * row_count)
    hidden_two = jnp.maximum(deconv_two + deconv2_bias, 0.0).astype(jnp.bfloat16)
    return (
        jnp.dot(
            lax.all_to_all(hidden_two, "mp", split_axis=2, concat_axis=3, tiled=True),
            final_weight,
            preferred_element_type=jnp.float32,
        )
        + final_bias
    ).astype(jnp.bfloat16)

LOG2E = 1.4426950408889634
MIB = 1024 * 1024
NT = (((1,), (1,)), ((), ()))


def dot_nt(left, right):
    return lax.dot_general(left, right, NT, preferred_element_type=jnp.float32)


def whole(shape):
    return pl.BlockSpec(shape, lambda *_: (0,) * len(shape))


def pack_kernel(
    query_ref, keys_ref, values_ref, resid_ref, out_ref, first_ref, last_ref, held_ref, done
):
    copies = []
    for index, source in enumerate((query_ref, keys_ref, values_ref)):
        for row in range(2):
            copy = pltpu.make_async_copy(source.at[0, row], held_ref.at[index, row], done.at[2 * index + row])
            copies.append(copy)
    copies.append(pltpu.make_async_copy(resid_ref.at[0, 0], first_ref, done.at[6]))
    copies.append(pltpu.make_async_copy(resid_ref.at[0, 1], last_ref, done.at[7]))
    for copy in copies:
        copy.start()
    for copy in copies[:6]:
        copy.wait()
    for head in range(out_ref.shape[0] // 2):
        lanes = pl.ds(128 * (head // 2), 128)
        own = slice(64 * (head % 2), 64 * (head % 2) + 64)
        for row in range(2):
            block = out_ref.at[2 * head + row]
            queries, keys, values = (held_ref[index, row, :, lanes][:, own] for index in range(3))
            block[0:32, :] = jnp.concatenate([queries[0:32], queries[32:64]], axis=1)
            block[32:96, :] = jnp.concatenate([keys, values], axis=1)
    for copy in copies[6:]:
        copy.wait()


def pack_tokens(query, keys, values, resid, device_count):
    edge = jax.ShapeDtypeStruct(resid.shape[2:], resid.dtype)
    return pl.pallas_call(
        pack_kernel,
        in_specs=[pl.BlockSpec(memory_space=pl.ANY)] * 4,
        out_shape=(jax.ShapeDtypeStruct((device_count, 96, 128), jnp.bfloat16), edge, edge),
        scratch_shapes=[pltpu.VMEM((3,) + query.shape[1:], jnp.bfloat16), pltpu.SemaphoreType.DMA((8,))],
        compiler_params=pltpu.CompilerParams(vmem_limit_bytes=60 * MIB),
        name="pack_tokens",
    )(query, keys, values, resid)


def reorder_kernel(weight_ref, after_ref, out_ref):
    del after_ref
    out_ref[0] = jnp.swapaxes(weight_ref[:, 0], 0, 1)


def reorder_taps(weight, rows, after):
    channels, _, columns, width = weight.shape
    block = channels // 2 if width > 1024 else channels

    def row_at(place):
        row = rows[0]
        for index in range(1, len(rows)):
            row = jnp.where(place == index, rows[index], row)
        return row

    moved = 2 * len(rows) * channels * columns * width * weight.dtype.itemsize
    return pl.pallas_call(
        reorder_kernel,
        grid=(len(rows), channels // block),
        in_specs=[
            pl.BlockSpec((block, 1, columns, width), lambda i, j: (j, row_at(i), 0, 0)),
            pl.BlockSpec(memory_space=pl.ANY),
        ],
        out_specs=pl.BlockSpec((1, columns, block, width), lambda i, j: (i, 0, j, 0)),
        out_shape=jax.ShapeDtypeStruct((len(rows), columns, channels, width), weight.dtype),
        compiler_params=pltpu.CompilerParams(vmem_limit_bytes=60 * MIB),
        cost_estimate=pl.CostEstimate(flops=0, bytes_accessed=moved, transcendentals=0),
        name="reorder_taps",
    )(weight, after)


def pair_kernel(weight_ref, after_ref, out_ref):
    del after_ref
    width = weight_ref.shape[3]
    taps = jnp.swapaxes(weight_ref[:, 0], 0, 1)
    for parity, columns in enumerate(((3, 1), (2, 0))):
        for place, column in enumerate(columns):
            out_ref[0, parity, :, place * width : (place + 1) * width] = taps[column]


def pair_taps(weight, after):
    channels, rows, columns, width = weight.shape
    moved = 2 * channels * rows * columns * width * weight.dtype.itemsize
    return pl.pallas_call(
        pair_kernel,
        grid=(rows,),
        in_specs=[
            pl.BlockSpec((channels, 1, columns, width), lambda i: (0, i, 0, 0)),
            pl.BlockSpec(memory_space=pl.ANY),
        ],
        out_specs=pl.BlockSpec((1, 2, channels, 2 * width), lambda i: (i, 0, 0, 0)),
        out_shape=jax.ShapeDtypeStruct((rows, 2, channels, 2 * width), weight.dtype),
        compiler_params=pltpu.CompilerParams(vmem_limit_bytes=60 * MIB),
        cost_estimate=pl.CostEstimate(flops=0, bytes_accessed=moved, transcendentals=0),
        name="pair_taps",
    )(weight, after)


def attend_kernel(parity_ref, own_ref, other_ref, out_ref, pairs_ref, values_ref, total_ref, mixed_ref, *, chunk):
    half = pairs_ref.shape[0] // 2
    count = 2 * half

    pairs_ref[0:half, :] = own_ref[:, 32:96, :].reshape(half, 128)
    pairs_ref[half:count, :] = other_ref[...].reshape(half, 128)
    longest = jnp.zeros((1, 1), jnp.float32)
    for start in range(0, count, 512):
        wide = pairs_ref[start : start + 512, :].astype(jnp.float32).T
        values_ref[:, start : start + 512] = wide[64:128].astype(jnp.bfloat16)
        norms = jnp.sum(wide[0:64] * wide[0:64], axis=0, keepdims=True)
        longest = jnp.maximum(longest, jnp.max(norms, axis=1, keepdims=True))

    sources = own_ref.shape[0]
    rows = sources * 32
    packed = own_ref[:, 0:32, :].reshape(rows, 128)
    wide = (packed.astype(jnp.float32) * HEAD_DIM ** (-0.5)).T
    zeros = jnp.zeros((64, rows), jnp.float32)
    exact = jnp.concatenate(
        [jnp.concatenate([wide[0:64], wide[64:128]], axis=1), jnp.concatenate([zeros, zeros], axis=1)], axis=0
    )
    queries = exact.astype(jnp.bfloat16)
    norms = jnp.sum(exact * exact, axis=0, keepdims=True)
    bound = 1.01 * jnp.max(norms * longest)
    small = bound <= 50.0 * 50.0

    @pl.when(small)
    def _():
        total, mixed = None, None
        for start in range(0, count, chunk):
            scores = jnp.dot(pairs_ref[start : start + chunk, :], queries, preferred_element_type=jnp.float32)
            exps = jnp.exp2(scores * LOG2E)
            part = jnp.sum(exps, axis=0, keepdims=True)
            product = jnp.dot(
                values_ref[:, start : start + chunk], exps.astype(jnp.bfloat16), preferred_element_type=jnp.float32
            )
            total = part if total is None else total + part
            mixed = product if mixed is None else mixed + product
        total_ref[...] = total
        mixed_ref[...] = mixed

    @pl.when(jnp.logical_not(small))
    def _():
        total_ref[...] = jnp.zeros_like(total_ref)
        mixed_ref[...] = jnp.zeros_like(mixed_ref)

        def absorb(index, top):
            start = pl.multiple_of(index * chunk, chunk)
            scores = jnp.dot(pairs_ref[pl.ds(start, chunk), :], queries, preferred_element_type=jnp.float32)
            fresh = jnp.maximum(top, jnp.max(scores, axis=0, keepdims=True))
            exps = jnp.exp2((scores - fresh) * LOG2E)
            shrink = jnp.exp2((top - fresh) * LOG2E)
            product = jnp.dot(
                values_ref[:, pl.ds(start, chunk)], exps.astype(jnp.bfloat16), preferred_element_type=jnp.float32
            )
            total_ref[...] = total_ref[...] * shrink + jnp.sum(exps, axis=0, keepdims=True)
            mixed_ref[...] = mixed_ref[...] * shrink + product
            return fresh

        lax.fori_loop(0, count // chunk, absorb, jnp.full((1, 2 * rows), -1e30, jnp.float32))

    attended = mixed_ref[...] / total_ref[...]
    joined = jnp.concatenate([attended[:, :rows], attended[:, rows:]], axis=0)
    rows = joined.T.astype(jnp.bfloat16).reshape(sources, 32, 128)
    rim = jnp.zeros((1, 32, 128), jnp.bfloat16)

    @pl.when(parity_ref[0] == 0)
    def _():
        out_ref[:, 0] = rows
        out_ref[:, 1] = jnp.concatenate([rows[1:], rim], axis=0)

    @pl.when(parity_ref[0] == 1)
    def _():
        out_ref[:, 0] = jnp.concatenate([rim, rows[:-1]], axis=0)
        out_ref[:, 1] = rows


def attend(parity, own, other, chunk=512):
    count = own.shape[0]
    return pl.pallas_call(
        functools.partial(attend_kernel, chunk=chunk),
        in_specs=[pl.BlockSpec(memory_space=pltpu.SMEM)] + [pl.BlockSpec(memory_space=pltpu.VMEM)] * 2,
        out_shape=jax.ShapeDtypeStruct((count, 2, 32, 128), jnp.bfloat16),
        scratch_shapes=[
            pltpu.VMEM((2 * count * 64, 128), jnp.bfloat16),
            pltpu.VMEM((64, 2 * count * 64), jnp.bfloat16),
            pltpu.VMEM((1, 64 * count), jnp.float32),
            pltpu.VMEM((64, 64 * count), jnp.float32),
        ],
        compiler_params=pltpu.CompilerParams(vmem_limit_bytes=40 * MIB),
        name="attend",
    )(parity, own, other)


def shift_columns(field, row_length):
    count = field.shape[0]
    column = lax.broadcasted_iota(jnp.int32, field.shape, 0) % row_length
    before = jnp.where(column == 0, 0.0, pltpu.roll(field, 1, 0))
    after = jnp.where(column == row_length - 1, 0.0, pltpu.roll(field, count - 1, 0))
    return before, after


def store_strided(wide_ref, start, value):
    for group in range(wide_ref.shape[0]):
        lanes = slice(128 * group, 128 * group + 128)
        wide_ref[group, pl.ds(start, value.shape[0], stride=2), :] = value[:, lanes]


def load_wide(wide_ref, rows):
    groups = [wide_ref[group, rows, :] for group in range(wide_ref.shape[0])]
    return jnp.concatenate(groups, axis=1).astype(jnp.bfloat16)


def attended_rows(mixed_ref):
    rows = []
    for parity, which in ((1, 0), (0, 0), (1, 1), (0, 1)):
        low, high = [], []
        for head in range(0, mixed_ref.shape[0], 2):
            left, right = mixed_ref[head, parity, which], mixed_ref[head + 1, parity, which]
            low.append(jnp.concatenate([left[:, :64], right[:, :64]], axis=1))
            high.append(jnp.concatenate([left[:, 64:], right[:, 64:]], axis=1))
        rows += [jnp.concatenate(low, axis=1), jnp.concatenate(high, axis=1)]
    return jnp.concatenate(rows, axis=0)


def head_kernel(
    inside_ref,
    mixed_ref,
    resid_ref,
    above_ref,
    below_ref,
    out_weight_ref,
    gain_ref,
    shift_ref,
    first_taps_ref,
    last_taps_ref,
    bias_one_ref,
    taps_two_ref,
    bias_two_ref,
    final_ref,
    final_bias_ref,
    out_ref,
    projection_ref,
    weight_one_ref,
    weight_two_ref,
    field_ref,
    sums_ref,
    wide_one_ref,
    copies_ref,
    wide_two_ref,
    heat_ref,
    held_ref,
    final_held_ref,
    done,
):
    channels = bias_one_ref.shape[0]
    slots = weight_one_ref.shape[0]
    ahead = slots - 1
    first = pltpu.make_async_copy(out_weight_ref, projection_ref, done.at[0])
    last = pltpu.make_async_copy(taps_two_ref, weight_two_ref, done.at[1])
    copies = []
    for index in range(4):
        source = first_taps_ref.at[index] if index < 3 else last_taps_ref.at[0]
        slot = index % slots
        copies.append(pltpu.make_async_copy(source, weight_one_ref.at[slot], done.at[2 + index]))
    near = pltpu.make_async_copy(resid_ref, held_ref, done.at[6])
    final = pltpu.make_async_copy(final_ref, final_held_ref, done.at[7])
    first.start()
    near.start()
    copies[0].start()

    attended = attended_rows(mixed_ref)
    first.wait()
    near.wait()
    for copy in copies[1:]:
        copy.start()
    last.start()
    final.start()
    projected = jnp.dot(attended, projection_ref[...], preferred_element_type=jnp.float32)
    for place, resid in enumerate((above_ref[...], held_ref[0], held_ref[1], below_ref[...])):
        rows = slice(64 * place, 64 * place + 64)
        stream = resid.astype(jnp.float32) + projected[rows]
        center = jnp.mean(stream, axis=-1, keepdims=True)
        shifted = stream - center
        variance = jnp.mean(shifted * shifted, axis=-1, keepdims=True)
        normed = shifted * lax.rsqrt(variance + EPSILON) * gain_ref[...][None, :] + shift_ref[...][None, :]
        if place in (0, 3):
            normed = jnp.where(inside_ref[place // 3] > 0, normed, 0.0)
        field_ref[rows, :] = normed.astype(jnp.bfloat16)

    for index, kernel_row in enumerate((1, 3, 2, 0)):
        copies[index].wait()
        if index == 3:
            last.wait()
            final.wait()
        low = 64 if kernel_row < 2 else 0
        weight = weight_one_ref[index % slots].reshape(4 * channels, weight_one_ref.shape[3])
        product = dot_nt(field_ref[low : low + 192, :], weight)
        parts = [product[:, channels * column : channels * (column + 1)] for column in range(4)]
        odd = shift_columns(parts[0], 64)[1] + parts[2]
        even = shift_columns(parts[3], 64)[0] + parts[1]
        if index % 2 == 0:
            sums_ref[0] = even
            sums_ref[1] = odd
        else:
            for parity in range(2):
                hidden = jnp.maximum((even, odd)[parity] + sums_ref[parity] + bias_one_ref[...][None, :], 0.0)
                for place in range(3):
                    row = 2 * place + (1 if index == 1 else 0)
                    value = hidden[64 * place : 64 * place + 64]
                    if row in (0, 5):
                        value = jnp.where(inside_ref[row // 5] > 0, value, 0.0)
                    store_strided(wide_one_ref, 128 * row + parity, value)

    hidden = load_wide(wide_one_ref, slice(None))
    before, after = shift_columns(hidden.astype(jnp.float32), 128)
    copies_ref[:, 0:channels] = before.astype(jnp.bfloat16)
    copies_ref[:, channels : 2 * channels] = hidden
    copies_ref[:, 2 * channels :] = after.astype(jnp.bfloat16)
    for row_parity in range(2):
        for parity in range(2):
            total = None
            lanes = slice(parity * channels, (parity + 2) * channels)
            for low, kernel_row in (((128, 1), (0, 3)), ((128, 2), (256, 0)))[row_parity]:
                product = dot_nt(copies_ref[low : low + 512, lanes], weight_two_ref[kernel_row, parity])
                total = product if total is None else total + product
            hidden = jnp.maximum(total + bias_two_ref[...][None, :], 0.0)
            for place in range(4):
                start = 256 * (2 * place + row_parity) + parity
                store_strided(wide_two_ref, start, hidden[128 * place : 128 * place + 128])
    for row in range(8):
        hidden = load_wide(wide_two_ref, slice(256 * row, 256 * row + 256))
        heat = dot_nt(final_held_ref[...], hidden) + final_bias_ref[...]
        heat_ref[row] = heat.astype(jnp.bfloat16)
    out_ref[...] = jnp.swapaxes(heat_ref[...], 0, 1)


def keypoint_head(
    inside,
    mixed,
    resid,
    above,
    below,
    out_weight,
    gain,
    shift,
    first_taps,
    last_taps,
    bias_one,
    taps_two,
    bias_two,
    final_weight,
    final_bias,
):
    width = resid.shape[-1]
    channels = bias_one.shape[0]
    keypoints = final_weight.shape[1]
    near = pl.BlockSpec(memory_space=pltpu.VMEM)
    far = pl.BlockSpec(memory_space=pl.ANY)
    return pl.pallas_call(
        head_kernel,
        in_specs=[pl.BlockSpec(memory_space=pltpu.SMEM), near, far, near, near, far, near, near]
        + [far, far, near, far, near, far, near],
        out_shape=jax.ShapeDtypeStruct((keypoints, 8, 256), jnp.bfloat16),
        scratch_shapes=[
            pltpu.VMEM(out_weight.shape, jnp.bfloat16),
            pltpu.VMEM((4, 4, channels, width), jnp.bfloat16),
            pltpu.VMEM((4, 2, channels, 2 * channels), jnp.bfloat16),
            pltpu.VMEM((256, width), jnp.bfloat16),
            pltpu.VMEM((2, 192, channels), jnp.float32),
            pltpu.VMEM((channels // 128, 768, 128), jnp.float32),
            pltpu.VMEM((768, 3 * channels), jnp.bfloat16),
            pltpu.VMEM((channels // 128, 2048, 128), jnp.float32),
            pltpu.VMEM((8, keypoints, 256), jnp.bfloat16),
            pltpu.VMEM(resid.shape, jnp.bfloat16),
            pltpu.VMEM((keypoints, channels), jnp.bfloat16),
            pltpu.SemaphoreType.DMA((8,)),
        ],
        compiler_params=pltpu.CompilerParams(vmem_limit_bytes=57 * MIB + MIB // 2),
        name="keypoint_head",
    )(
        inside,
        mixed,
        resid,
        above,
        below,
        out_weight,
        gain,
        shift,
        first_taps,
        last_taps,
        bias_one,
        taps_two,
        bias_two,
        final_weight.T,
        final_bias.reshape(-1, 1),
    )


def by_heads(
    query,
    keys,
    values,
    resid,
    out_weight,
    norm_gain,
    norm_bias,
    deconv1_weight,
    deconv1_bias,
    deconv2_weight,
    deconv2_bias,
    final_weight,
    final_bias,
):
    count = lax.axis_size("seq")
    place = lax.axis_index("seq")
    up = [(i, i + 1) for i in range(count - 1)]
    down = [(i + 1, i) for i in range(count - 1)]
    swap = [(i, i ^ 1) for i in range(count)]

    packed, first_row, last_row = pack_tokens(query, keys, values, resid, count)
    own = lax.all_to_all(packed, "seq", 0, 0, tiled=True)
    above = lax.ppermute(last_row, "seq", up)
    below = lax.ppermute(first_row, "seq", down)
    first_taps = reorder_taps(deconv1_weight, (1, 3, 2), packed)
    own, above, below, first_taps = lax.optimization_barrier((own, above, below, first_taps))
    other = lax.ppermute(own[:, 32:96], "seq", swap)
    sent = attend((place % 2).astype(jnp.int32).reshape(1), own, other)
    last_taps = reorder_taps(deconv1_weight, (0,), sent)
    taps_two = pair_taps(deconv2_weight, sent)
    back = lax.all_to_all(sent, "seq", 0, 0, tiled=True)
    back = back.reshape(count // 2, 2, 2, 32, 128)

    inside = jnp.stack([place > 0, place < count - 1]).astype(jnp.int32)
    heat = keypoint_head(
        inside,
        back,
        resid[0],
        above,
        below,
        out_weight,
        norm_gain,
        norm_bias,
        first_taps,
        last_taps,
        deconv1_bias,
        taps_two,
        deconv2_bias,
        final_weight,
        final_bias,
    )
    return jnp.transpose(heat, (1, 2, 0))[None]


def step(*arrays):
    query = arrays[0]
    frames, rows, columns, width = query.shape
    heads = width // HEAD_DIM
    whole_heads = lax.axis_size("mp") == 1 and lax.axis_size("seq") == 2 * heads
    if whole_heads and (frames, rows, columns) == (1, 2, 64):
        return by_heads(*arrays)
    return local(*arrays)


def solution(mesh):
    placed = (
        P(None, "seq", None, "mp"),
        P(None, "seq", None, "mp"),
        P(None, "seq", None, "mp"),
        P(None, "seq", "mp", None),
        P("mp", None),
        P(),
        P(),
        P("mp", None, None, None),
        P("mp"),
        P("mp", None, None, None),
        P("mp"),
        P(),
        P(),
    )
    return jax.shard_map(
        step, mesh=mesh, in_specs=placed, out_specs=P(None, "seq", "mp", None), check_vma=False
    )
```

```python
import functools

import jax
import jax.numpy as jnp
from jax import lax
from jax.experimental import pallas as pl
from jax.experimental.pallas import tpu as pltpu
from jax.sharding import PartitionSpec as P

HEAD_DIM = 64


TAP_TABLE = (((1, 1), (0, 3)), ((2, 0), (1, 2)))
EPSILON = 1e-06


def with_halo(array, sides, width):
    for axis, dim in sides:
        size, length = (lax.axis_size(axis), array.shape[dim])
        up = [(i, (i + 1) % size) for i in range(size - 1)]
        down = [(j, i) for i, j in up]
        last = lax.slice_in_dim(array, length - width, length, axis=dim)
        first = lax.slice_in_dim(array, 0, width, axis=dim)
        before = lax.ppermute(last, axis, up)
        after = lax.ppermute(first, axis, down)
        array = jnp.concatenate([before, array, after], axis=dim)
    return array


def tap_product(window, weight, kernel_row, kernel_col):
    tap = weight[:, kernel_row, kernel_col, :]
    return lax.dot_general(
        window, tap, (((3,), (1,)), ((), ())), preferred_element_type=jnp.float32
    )


def half_rows(padded, weight, tap_pairs, first_row, row_count):
    col_count = padded.shape[2] - 2
    halves = []
    for col_parity in range(2):
        summed = None
        for pad_row, kernel_row in tap_pairs:
            for pad_col, kernel_col in TAP_TABLE[col_parity]:
                window = padded[
                    :,
                    first_row + pad_row : first_row + pad_row + row_count,
                    pad_col : pad_col + col_count,
                    :,
                ]
                product = tap_product(window, weight, kernel_row, kernel_col)
                summed = product if summed is None else summed + product
        halves.append(summed)
    stacked = jnp.stack(halves, axis=3)
    return stacked.reshape(stacked.shape[0], row_count, 2 * col_count, stacked.shape[-1])


def upsample(padded, weight, row_count):
    even_rows = half_rows(padded, weight, TAP_TABLE[0], 0, row_count)
    odd_rows = half_rows(padded, weight, TAP_TABLE[1], 0, row_count)
    stacked = jnp.stack([even_rows, odd_rows], axis=2)
    return stacked.reshape(stacked.shape[0], 2 * row_count, stacked.shape[3], stacked.shape[4])


def pad_columns(field):
    return jnp.pad(field, ((0, 0), (0, 0), (1, 1), (0, 0)))


def layer_norm(stream, norm_gain, norm_bias):
    center = jnp.mean(stream, axis=-1, keepdims=True)
    shifted = stream - center
    variance = jnp.mean(shifted * shifted, axis=-1, keepdims=True)
    return (shifted * lax.rsqrt(variance + EPSILON) * norm_gain + norm_bias).astype(jnp.bfloat16)


def local(
    query,
    keys,
    values,
    resid,
    out_weight,
    norm_gain,
    norm_bias,
    deconv1_weight,
    deconv1_bias,
    deconv2_weight,
    deconv2_bias,
    final_weight,
    final_bias,
):
    frame_count, row_count, col_count, feature_width = query.shape
    local_heads = feature_width // HEAD_DIM
    score_scale = HEAD_DIM ** (-0.5)
    query_count = row_count * col_count
    queries = query.reshape(frame_count, query_count, local_heads, HEAD_DIM)
    start_max = jnp.full((frame_count, query_count, local_heads), -1e30, jnp.float32)
    running_max = start_max
    key_piece = lax.all_gather(keys, "seq", axis=1, tiled=True).reshape(
        frame_count, -1, local_heads, HEAD_DIM
    )
    value_piece = lax.all_gather(values, "seq", axis=1, tiled=True).reshape(
        frame_count, -1, local_heads, HEAD_DIM
    )
    scores = (
        jnp.einsum("fqhd,fkhd->fqhk", queries, key_piece, preferred_element_type=jnp.float32)
        * score_scale
    )
    fresh_max = jnp.maximum(running_max, jnp.max(scores, axis=-1))
    exps = jnp.exp(scores - fresh_max[..., None])
    denominator = jnp.sum(exps, axis=-1)
    weighted = jnp.einsum(
        "fqhk,fkhd->fqhd",
        exps.astype(jnp.bfloat16),
        value_piece,
        preferred_element_type=jnp.float32,
    )
    running_max, denominator, weighted = (fresh_max, denominator, weighted)
    attended = (
        (weighted / denominator[..., None])
        .astype(jnp.bfloat16)
        .reshape(frame_count, row_count, col_count, feature_width)
    )
    partial_value = jnp.dot(attended, out_weight, preferred_element_type=jnp.float32)
    summed = lax.psum(partial_value.astype(jnp.bfloat16), "mp").astype(jnp.float32)
    full_resid = lax.all_gather(resid, "mp", axis=2, tiled=True)
    normed = layer_norm(full_resid.astype(jnp.float32) + summed, norm_gain, norm_bias)
    rimmed = with_halo(normed, (("seq", 1),), 1)
    padded = pad_columns(rimmed)
    deconv_one = upsample(padded, deconv1_weight, row_count)
    hidden_one = jnp.maximum(deconv_one + deconv1_bias, 0.0).astype(jnp.bfloat16)
    gathered = lax.all_gather(hidden_one, "mp", axis=3, tiled=True)
    middle = with_halo(gathered, (("seq", 1),), 1)
    deconv_two = upsample(pad_columns(middle), deconv2_weight, 2 * row_count)
    hidden_two = jnp.maximum(deconv_two + deconv2_bias, 0.0).astype(jnp.bfloat16)
    return (
        jnp.dot(
            lax.all_to_all(hidden_two, "mp", split_axis=2, concat_axis=3, tiled=True),
            final_weight,
            preferred_element_type=jnp.float32,
        )
        + final_bias
    ).astype(jnp.bfloat16)

LOG2E = 1.4426950408889634
MIB = 1024 * 1024
NT = (((1,), (1,)), ((), ()))


def dot_nt(left, right):
    return lax.dot_general(left, right, NT, preferred_element_type=jnp.float32)


def whole(shape):
    return pl.BlockSpec(shape, lambda *_: (0,) * len(shape))


def pack_kernel(
    query_ref, keys_ref, values_ref, resid_ref, out_ref, first_ref, last_ref, held_ref, done
):
    copies = []
    for index, source in enumerate((query_ref, keys_ref, values_ref)):
        for row in range(2):
            copy = pltpu.make_async_copy(source.at[0, row], held_ref.at[index, row], done.at[2 * index + row])
            copies.append(copy)
    copies.append(pltpu.make_async_copy(resid_ref.at[0, 0], first_ref, done.at[6]))
    copies.append(pltpu.make_async_copy(resid_ref.at[0, 1], last_ref, done.at[7]))
    for copy in copies:
        copy.start()
    for copy in copies[:6]:
        copy.wait()
    for head in range(out_ref.shape[0] // 2):
        lanes = pl.ds(128 * (head // 2), 128)
        own = slice(64 * (head % 2), 64 * (head % 2) + 64)
        for row in range(2):
            block = out_ref.at[2 * head + row]
            queries, keys, values = (held_ref[index, row, :, lanes][:, own] for index in range(3))
            block[0:32, :] = jnp.concatenate([queries[0:32], queries[32:64]], axis=1)
            block[32:96, :] = jnp.concatenate([keys, values], axis=1)
    for copy in copies[6:]:
        copy.wait()


def pack_tokens(query, keys, values, resid, device_count):
    edge = jax.ShapeDtypeStruct(resid.shape[2:], resid.dtype)
    return pl.pallas_call(
        pack_kernel,
        in_specs=[pl.BlockSpec(memory_space=pl.ANY)] * 4,
        out_shape=(jax.ShapeDtypeStruct((device_count, 96, 128), jnp.bfloat16), edge, edge),
        scratch_shapes=[pltpu.VMEM((3,) + query.shape[1:], jnp.bfloat16), pltpu.SemaphoreType.DMA((8,))],
        compiler_params=pltpu.CompilerParams(vmem_limit_bytes=60 * MIB),
        name="pack_tokens",
    )(query, keys, values, resid)


def reorder_kernel(weight_ref, after_ref, out_ref):
    del after_ref
    out_ref[0] = jnp.swapaxes(weight_ref[:, 0], 0, 1)


def reorder_taps(weight, rows, after):
    channels, _, columns, width = weight.shape
    block = channels // 2 if width > 1024 else channels

    def row_at(place):
        row = rows[0]
        for index in range(1, len(rows)):
            row = jnp.where(place == index, rows[index], row)
        return row

    moved = 2 * len(rows) * channels * columns * width * weight.dtype.itemsize
    return pl.pallas_call(
        reorder_kernel,
        grid=(len(rows), channels // block),
        in_specs=[
            pl.BlockSpec((block, 1, columns, width), lambda i, j: (j, row_at(i), 0, 0)),
            pl.BlockSpec(memory_space=pl.ANY),
        ],
        out_specs=pl.BlockSpec((1, columns, block, width), lambda i, j: (i, 0, j, 0)),
        out_shape=jax.ShapeDtypeStruct((len(rows), columns, channels, width), weight.dtype),
        compiler_params=pltpu.CompilerParams(vmem_limit_bytes=60 * MIB),
        cost_estimate=pl.CostEstimate(flops=0, bytes_accessed=moved, transcendentals=0),
        name="reorder_taps",
    )(weight, after)


def pair_kernel(weight_ref, after_ref, out_ref):
    del after_ref
    width = weight_ref.shape[3]
    taps = jnp.swapaxes(weight_ref[:, 0], 0, 1)
    for parity, columns in enumerate(((3, 1), (2, 0))):
        for place, column in enumerate(columns):
            out_ref[0, parity, :, place * width : (place + 1) * width] = taps[column]


def pair_taps(weight, after):
    channels, rows, columns, width = weight.shape
    moved = 2 * channels * rows * columns * width * weight.dtype.itemsize
    return pl.pallas_call(
        pair_kernel,
        grid=(rows,),
        in_specs=[
            pl.BlockSpec((channels, 1, columns, width), lambda i: (0, i, 0, 0)),
            pl.BlockSpec(memory_space=pl.ANY),
        ],
        out_specs=pl.BlockSpec((1, 2, channels, 2 * width), lambda i: (i, 0, 0, 0)),
        out_shape=jax.ShapeDtypeStruct((rows, 2, channels, 2 * width), weight.dtype),
        compiler_params=pltpu.CompilerParams(vmem_limit_bytes=60 * MIB),
        cost_estimate=pl.CostEstimate(flops=0, bytes_accessed=moved, transcendentals=0),
        name="pair_taps",
    )(weight, after)


def attend_kernel(parity_ref, own_ref, other_ref, out_ref, pairs_ref, values_ref, total_ref, mixed_ref, *, chunk):
    half = pairs_ref.shape[0] // 2
    count = 2 * half

    pairs_ref[0:half, :] = own_ref[:, 32:96, :].reshape(half, 128)
    pairs_ref[half:count, :] = other_ref[...].reshape(half, 128)
    longest = jnp.zeros((1, 1), jnp.float32)
    for start in range(0, count, 512):
        wide = pairs_ref[start : start + 512, :].astype(jnp.float32).T
        values_ref[:, start : start + 512] = wide[64:128].astype(jnp.bfloat16)
        norms = jnp.sum(wide[0:64] * wide[0:64], axis=0, keepdims=True)
        longest = jnp.maximum(longest, jnp.max(norms, axis=1, keepdims=True))

    sources = own_ref.shape[0]
    rows = sources * 32
    packed = own_ref[:, 0:32, :].reshape(rows, 128)
    wide = (packed.astype(jnp.float32) * HEAD_DIM ** (-0.5)).T
    zeros = jnp.zeros((64, rows), jnp.float32)
    exact = jnp.concatenate(
        [jnp.concatenate([wide[0:64], wide[64:128]], axis=1), jnp.concatenate([zeros, zeros], axis=1)], axis=0
    )
    queries = exact.astype(jnp.bfloat16)
    norms = jnp.sum(exact * exact, axis=0, keepdims=True)
    bound = 1.01 * jnp.max(norms * longest)
    small = bound <= 50.0 * 50.0

    @pl.when(small)
    def _():
        total, mixed = None, None
        for start in range(0, count, chunk):
            scores = jnp.dot(pairs_ref[start : start + chunk, :], queries, preferred_element_type=jnp.float32)
            exps = jnp.exp2(scores * LOG2E)
            part = jnp.sum(exps, axis=0, keepdims=True)
            product = jnp.dot(
                values_ref[:, start : start + chunk], exps.astype(jnp.bfloat16), preferred_element_type=jnp.float32
            )
            total = part if total is None else total + part
            mixed = product if mixed is None else mixed + product
        total_ref[...] = total
        mixed_ref[...] = mixed

    @pl.when(jnp.logical_not(small))
    def _():
        total_ref[...] = jnp.zeros_like(total_ref)
        mixed_ref[...] = jnp.zeros_like(mixed_ref)

        def absorb(index, top):
            start = pl.multiple_of(index * chunk, chunk)
            scores = jnp.dot(pairs_ref[pl.ds(start, chunk), :], queries, preferred_element_type=jnp.float32)
            fresh = jnp.maximum(top, jnp.max(scores, axis=0, keepdims=True))
            exps = jnp.exp2((scores - fresh) * LOG2E)
            shrink = jnp.exp2((top - fresh) * LOG2E)
            product = jnp.dot(
                values_ref[:, pl.ds(start, chunk)], exps.astype(jnp.bfloat16), preferred_element_type=jnp.float32
            )
            total_ref[...] = total_ref[...] * shrink + jnp.sum(exps, axis=0, keepdims=True)
            mixed_ref[...] = mixed_ref[...] * shrink + product
            return fresh

        lax.fori_loop(0, count // chunk, absorb, jnp.full((1, 2 * rows), -1e30, jnp.float32))

    attended = mixed_ref[...] / total_ref[...]
    joined = jnp.concatenate([attended[:, :rows], attended[:, rows:]], axis=0)
    rows = joined.T.astype(jnp.bfloat16).reshape(sources, 32, 128)
    rim = jnp.zeros((1, 32, 128), jnp.bfloat16)

    @pl.when(parity_ref[0] == 0)
    def _():
        out_ref[:, 0] = rows
        out_ref[:, 1] = jnp.concatenate([rows[1:], rim], axis=0)

    @pl.when(parity_ref[0] == 1)
    def _():
        out_ref[:, 0] = jnp.concatenate([rim, rows[:-1]], axis=0)
        out_ref[:, 1] = rows


def attend(parity, own, other, chunk=512):
    count = own.shape[0]
    return pl.pallas_call(
        functools.partial(attend_kernel, chunk=chunk),
        in_specs=[pl.BlockSpec(memory_space=pltpu.SMEM)] + [pl.BlockSpec(memory_space=pltpu.VMEM)] * 2,
        out_shape=jax.ShapeDtypeStruct((count, 2, 32, 128), jnp.bfloat16),
        scratch_shapes=[
            pltpu.VMEM((2 * count * 64, 128), jnp.bfloat16),
            pltpu.VMEM((64, 2 * count * 64), jnp.bfloat16),
            pltpu.VMEM((1, 64 * count), jnp.float32),
            pltpu.VMEM((64, 64 * count), jnp.float32),
        ],
        compiler_params=pltpu.CompilerParams(vmem_limit_bytes=40 * MIB),
        name="attend",
    )(parity, own, other)


def shift_columns(field, row_length):
    count = field.shape[0]
    column = lax.broadcasted_iota(jnp.int32, field.shape, 0) % row_length
    before = jnp.where(column == 0, 0.0, pltpu.roll(field, 1, 0))
    after = jnp.where(column == row_length - 1, 0.0, pltpu.roll(field, count - 1, 0))
    return before, after


def store_strided(wide_ref, start, value):
    for group in range(wide_ref.shape[0]):
        lanes = slice(128 * group, 128 * group + 128)
        wide_ref[group, pl.ds(start, value.shape[0], stride=2), :] = value[:, lanes]


def load_wide(wide_ref, rows):
    groups = [wide_ref[group, rows, :] for group in range(wide_ref.shape[0])]
    return jnp.concatenate(groups, axis=1).astype(jnp.bfloat16)


def attended_rows(mixed_ref):
    rows = []
    for parity, which in ((1, 0), (0, 0), (1, 1), (0, 1)):
        low, high = [], []
        for head in range(0, mixed_ref.shape[0], 2):
            left, right = mixed_ref[head, parity, which], mixed_ref[head + 1, parity, which]
            low.append(jnp.concatenate([left[:, :64], right[:, :64]], axis=1))
            high.append(jnp.concatenate([left[:, 64:], right[:, 64:]], axis=1))
        rows += [jnp.concatenate(low, axis=1), jnp.concatenate(high, axis=1)]
    return jnp.concatenate(rows, axis=0)


def head_kernel(
    inside_ref,
    mixed_ref,
    resid_ref,
    above_ref,
    below_ref,
    out_weight_ref,
    gain_ref,
    shift_ref,
    first_taps_ref,
    last_taps_ref,
    bias_one_ref,
    taps_two_ref,
    bias_two_ref,
    final_ref,
    final_bias_ref,
    out_ref,
    projection_ref,
    weight_one_ref,
    weight_two_ref,
    field_ref,
    sums_ref,
    wide_one_ref,
    copies_ref,
    wide_two_ref,
    heat_ref,
    held_ref,
    done,
):
    channels = bias_one_ref.shape[0]
    slots = weight_one_ref.shape[0]
    ahead = slots - 1
    first = pltpu.make_async_copy(out_weight_ref, projection_ref, done.at[0])
    last = pltpu.make_async_copy(taps_two_ref, weight_two_ref, done.at[1])
    copies = []
    for index in range(4):
        source = first_taps_ref.at[index] if index < 3 else last_taps_ref.at[0]
        slot = index % slots
        copies.append(pltpu.make_async_copy(source, weight_one_ref.at[slot], done.at[2 + index]))
    near = pltpu.make_async_copy(resid_ref, held_ref, done.at[6])
    first.start()
    near.start()
    copies[0].start()

    attended = attended_rows(mixed_ref)
    first.wait()
    near.wait()
    for copy in copies[1:]:
        copy.start()
    last.start()
    projected = jnp.dot(attended, projection_ref[...], preferred_element_type=jnp.float32)
    for place, resid in enumerate((above_ref[...], held_ref[0], held_ref[1], below_ref[...])):
        rows = slice(64 * place, 64 * place + 64)
        stream = resid.astype(jnp.float32) + projected[rows]
        center = jnp.mean(stream, axis=-1, keepdims=True)
        shifted = stream - center
        variance = jnp.mean(shifted * shifted, axis=-1, keepdims=True)
        normed = shifted * lax.rsqrt(variance + EPSILON) * gain_ref[...][None, :] + shift_ref[...][None, :]
        if place in (0, 3):
            normed = jnp.where(inside_ref[place // 3] > 0, normed, 0.0)
        field_ref[rows, :] = normed.astype(jnp.bfloat16)

    for index, kernel_row in enumerate((1, 3, 2, 0)):
        copies[index].wait()
        if index == 3:
            last.wait()
        low = 64 if kernel_row < 2 else 0
        weight = weight_one_ref[index % slots].reshape(4 * channels, weight_one_ref.shape[3])
        product = dot_nt(field_ref[low : low + 192, :], weight)
        parts = [product[:, channels * column : channels * (column + 1)] for column in range(4)]
        odd = shift_columns(parts[0], 64)[1] + parts[2]
        even = shift_columns(parts[3], 64)[0] + parts[1]
        if index % 2 == 0:
            sums_ref[0] = even
            sums_ref[1] = odd
        else:
            for parity in range(2):
                hidden = jnp.maximum((even, odd)[parity] + sums_ref[parity] + bias_one_ref[...][None, :], 0.0)
                for place in range(3):
                    row = 2 * place + (1 if index == 1 else 0)
                    value = hidden[64 * place : 64 * place + 64]
                    if row in (0, 5):
                        value = jnp.where(inside_ref[row // 5] > 0, value, 0.0)
                    store_strided(wide_one_ref, 128 * row + parity, value)

    hidden = load_wide(wide_one_ref, slice(None))
    before, after = shift_columns(hidden.astype(jnp.float32), 128)
    copies_ref[:, 0:channels] = before.astype(jnp.bfloat16)
    copies_ref[:, channels : 2 * channels] = hidden
    copies_ref[:, 2 * channels :] = after.astype(jnp.bfloat16)
    for row_parity in range(2):
        for parity in range(2):
            total = None
            lanes = slice(parity * channels, (parity + 2) * channels)
            for low, kernel_row in (((128, 1), (0, 3)), ((128, 2), (256, 0)))[row_parity]:
                product = dot_nt(copies_ref[low : low + 512, lanes], weight_two_ref[kernel_row, parity])
                total = product if total is None else total + product
            hidden = jnp.maximum(total + bias_two_ref[...][None, :], 0.0)
            for place in range(4):
                start = 256 * (2 * place + row_parity) + parity
                store_strided(wide_two_ref, start, hidden[128 * place : 128 * place + 128])
    for row in range(8):
        hidden = load_wide(wide_two_ref, slice(256 * row, 256 * row + 256))
        heat = dot_nt(final_ref[...], hidden) + final_bias_ref[...]
        heat_ref[row] = heat.astype(jnp.bfloat16)
    out_ref[...] = jnp.swapaxes(heat_ref[...], 0, 1)


def keypoint_head(
    inside,
    mixed,
    resid,
    above,
    below,
    out_weight,
    gain,
    shift,
    first_taps,
    last_taps,
    bias_one,
    taps_two,
    bias_two,
    final_weight,
    final_bias,
):
    width = resid.shape[-1]
    channels = bias_one.shape[0]
    keypoints = final_weight.shape[1]
    near = pl.BlockSpec(memory_space=pltpu.VMEM)
    far = pl.BlockSpec(memory_space=pl.ANY)
    return pl.pallas_call(
        head_kernel,
        in_specs=[pl.BlockSpec(memory_space=pltpu.SMEM), near, far, near, near, far, near, near]
        + [far, far, near, far, near, near, near],
        out_shape=jax.ShapeDtypeStruct((keypoints, 8, 256), jnp.bfloat16),
        scratch_shapes=[
            pltpu.VMEM(out_weight.shape, jnp.bfloat16),
            pltpu.VMEM((4, 4, channels, width), jnp.bfloat16),
            pltpu.VMEM((4, 2, channels, 2 * channels), jnp.bfloat16),
            pltpu.VMEM((256, width), jnp.bfloat16),
            pltpu.VMEM((2, 192, channels), jnp.float32),
            pltpu.VMEM((channels // 128, 768, 128), jnp.float32),
            pltpu.VMEM((768, 3 * channels), jnp.bfloat16),
            pltpu.VMEM((channels // 128, 2048, 128), jnp.float32),
            pltpu.VMEM((8, keypoints, 256), jnp.bfloat16),
            pltpu.VMEM(resid.shape, jnp.bfloat16),
            pltpu.SemaphoreType.DMA((7,)),
        ],
        compiler_params=pltpu.CompilerParams(vmem_limit_bytes=57 * MIB + MIB // 2),
        name="keypoint_head",
    )(
        inside,
        mixed,
        resid,
        above,
        below,
        out_weight,
        gain,
        shift,
        first_taps,
        last_taps,
        bias_one,
        taps_two,
        bias_two,
        final_weight.T,
        final_bias.reshape(-1, 1),
    )


def by_heads(
    query,
    keys,
    values,
    resid,
    out_weight,
    norm_gain,
    norm_bias,
    deconv1_weight,
    deconv1_bias,
    deconv2_weight,
    deconv2_bias,
    final_weight,
    final_bias,
):
    count = lax.axis_size("seq")
    place = lax.axis_index("seq")
    up = [(i, i + 1) for i in range(count - 1)]
    down = [(i + 1, i) for i in range(count - 1)]
    swap = [(i, i ^ 1) for i in range(count)]

    packed, first_row, last_row = pack_tokens(query, keys, values, resid, count)
    own = lax.all_to_all(packed, "seq", 0, 0, tiled=True)
    above = lax.ppermute(last_row, "seq", up)
    below = lax.ppermute(first_row, "seq", down)
    first_taps = reorder_taps(deconv1_weight, (1, 3, 2), packed)
    own, above, below, first_taps = lax.optimization_barrier((own, above, below, first_taps))
    other = lax.ppermute(own[:, 32:96], "seq", swap)
    sent = attend((place % 2).astype(jnp.int32).reshape(1), own, other)
    last_taps = reorder_taps(deconv1_weight, (0,), sent)
    taps_two = pair_taps(deconv2_weight, sent)
    back = lax.all_to_all(sent, "seq", 0, 0, tiled=True)
    back = back.reshape(count // 2, 2, 2, 32, 128)

    inside = jnp.stack([place > 0, place < count - 1]).astype(jnp.int32)
    heat = keypoint_head(
        inside,
        back,
        resid[0],
        above,
        below,
        out_weight,
        norm_gain,
        norm_bias,
        first_taps,
        last_taps,
        deconv1_bias,
        taps_two,
        deconv2_bias,
        final_weight,
        final_bias,
    )
    return jnp.transpose(heat, (1, 2, 0))[None]


def step(*arrays):
    query = arrays[0]
    frames, rows, columns, width = query.shape
    heads = width // HEAD_DIM
    whole_heads = lax.axis_size("mp") == 1 and lax.axis_size("seq") == 2 * heads
    if whole_heads and (frames, rows, columns) == (1, 2, 64):
        return by_heads(*arrays)
    return local(*arrays)


def solution(mesh):
    placed = (
        P(None, "seq", None, "mp"),
        P(None, "seq", None, "mp"),
        P(None, "seq", None, "mp"),
        P(None, "seq", "mp", None),
        P("mp", None),
        P(),
        P(),
        P("mp", None, None, None),
        P("mp"),
        P("mp", None, None, None),
        P("mp"),
        P(),
        P(),
    )
    return jax.shard_map(
        step, mesh=mesh, in_specs=placed, out_specs=P(None, "seq", "mp", None), check_vma=False
    )
```
